512 devices in a mesh: tm: 32 (over x, y, core), space: 16 (over z).
Axes of the slice: x: 4, y: 4, z: 16, core: 2. Of those that a mesh axis runs over, the one named last changes fastest.
Arguments:
- latent: float32 [128, 512, 1024], P('tm', 'space'), may hold values from -3 to 3
- counts: int32 [128, 512, 1024], P('tm', 'space'), may hold values from 0 to 6
- exposure: float32 [128, 512, 1024], P('tm', 'space'), may hold values from 0.5 to 6, as said below
- region_ids: int32 [128], P('space'), may hold values from 0 to 15
- coefficients: float32 [16], replicated, may hold values from -2 to 2
Outputs:
- updated: float32 [128, 512, 1024], P('tm', 'space')
- residual: float32 [128, 512, 1024], P('tm', 'space')
The draws below stay inside these ranges and needn't reach their ends.
Inputs may be any that keep to these rules, and one draw needn't show every extreme that they name: exposure is positive.
All inputs are finite; a program needn't handle non-finite values.
Results may differ from the reference program's by a relative error of at most 0.00013.
Values sent between devices are 32-bit elements; how exact they have to be, the bound alone decides.
No kernel may reach another device: no remote copies, remote signals or barrier semaphores. Data moves between devices by JAX's collectives and lax.ppermute only.
A program may use at most 64 MiB of HBM per device.

```python
import jax
import jax.numpy as jnp

COLS = 1024
REGION_ROWS = 4
REGIONS = 16
ITERS = 2
NT = 128
NR = 512


def draw_exposure(key, part):
    key = jax.random.fold_in(key, 11)
    share = (jnp.arange(NT, dtype=jnp.float32) / max(NT - 1, 1))[:, None, None]
    trend = jnp.exp(jnp.log(3.0) * share)
    spread = jax.random.uniform(key, (NT, NR, COLS), jnp.float32, jnp.log(0.5), jnp.log(2.0))
    return trend * jnp.exp(spread)


def touch_ends(drawn, own_key, smallest, high):
    index_at = [jax.random.randint(jax.random.fold_in(own_key, axis), (), 0, length) for axis, length in enumerate(drawn.shape)]
    widest = drawn.shape.index(max(drawn.shape))
    beside = index_at[:widest] + [(index_at[widest] + 1) % drawn.shape[widest]] + index_at[widest + 1:]
    return drawn.at[tuple(index_at)].set(smallest).at[tuple(beside)].set(high)


def block_scale(stream_key, shape, cuts, low, high):
    level, own = 1.0, jax.random.fold_in(stream_key, 6)
    for axis_at, parts in cuts:
        heights = jnp.exp(jax.random.uniform(jax.random.fold_in(own, axis_at), (parts,), jnp.float32, low / len(cuts), high / len(cuts)))
        level = level * jnp.repeat(heights, shape[axis_at] // parts).reshape([-1 if axis == axis_at else 1 for axis in range(len(shape))])
    return level


def centred(key, shape, width, limit, pieces=(), kind=jnp.bfloat16):
    level = block_scale(key, shape, pieces, -0.22, 0.18) if pieces else 1.0
    entries = jax.random.normal(key, shape, jnp.float32) * width * level
    return jnp.minimum(jnp.maximum(entries, -limit), limit).astype(kind)


def setup_inputs(seed: int = 0) -> dict:
    key_list = jax.random.split(jax.random.key(seed), 6)
    latent = centred(key_list[0], (NT, NR, COLS), 0.5, 3.0, ((0, 32), (1, 16)), jnp.float32)
    counts = touch_ends(jax.random.randint(key_list[1], (NT, NR, COLS), 0, 7), jax.random.fold_in(key_list[1], 1), 0, 6).astype(jnp.int32)
    exposure = draw_exposure(jax.random.fold_in(key_list[5], 71), 0)
    region_ids = touch_ends(jax.random.randint(key_list[3], (NR // REGION_ROWS,), 0, REGIONS), jax.random.fold_in(key_list[3], 1), 0, REGIONS - 1).astype(jnp.int32)
    coefficients = centred(key_list[4], (REGIONS,), 0.5, 2.0, (), jnp.float32)
    return dict(latent=latent, counts=counts, exposure=exposure, region_ids=region_ids, coefficients=coefficients)


kappa_square = 0.3
time_corr = 0.9
prior_scale = 0.05


def stiffness(field):
    padded = jnp.pad(field, ((0, 0), (1, 1), (1, 1)))
    neighbours = padded[:, 2:, 1:-1] + padded[:, :-2, 1:-1] + padded[:, 1:-1, 2:] + padded[:, 1:-1, :-2]
    return (kappa_square + 4.0) * field - neighbours


def precision(field):
    spatial = stiffness(stiffness(field))
    padded = jnp.pad(spatial, ((1, 1), (0, 0), (0, 0)))
    day_index = jnp.arange(NT)
    weight = jnp.where((day_index == 0) | (day_index == NT - 1), 1.0, 1.0 + time_corr * time_corr)
    weight = weight.astype(jnp.float32)[:, None, None]
    return prior_scale * (weight * spatial - time_corr * (padded[:-2] + padded[2:]))


def reference(latent, counts, exposure, region_ids, coefficients):
    offset = jnp.repeat(coefficients[region_ids], REGION_ROWS)
    intensity = exposure * jnp.exp(offset[None, :, None] + latent)
    gradient = precision(latent) - counts.astype(jnp.float32) + intensity
    newton_step = jnp.zeros_like(latent)
    residual = -gradient
    direction = residual
    norm_now = jnp.sum(residual * residual)
    for iteration in range(ITERS):
        image_vec = precision(direction) + intensity * direction
        step_size = norm_now / jnp.sum(direction * image_vec)
        newton_step = newton_step + step_size * direction
        residual = residual - step_size * image_vec
        if iteration + 1 < ITERS:
            norm_next = jnp.sum(residual * residual)
            direction = residual + (norm_next / norm_now) * direction
            norm_now = norm_next
    return latent + newton_step, residual
```

```python
import jax
import jax.numpy as jnp
from jax import lax
from jax.sharding import PartitionSpec as P

kappa_square = 0.3
time_corr = 0.9
prior_scale = 0.05

COUPLE = prior_scale * time_corr
INNER = prior_scale * (1.0 + time_corr * time_corr)


def exchange(up_edge, down_edge, axis):
    count = lax.axis_size(axis)
    before = lax.ppermute(down_edge, axis, [(i, i + 1) for i in range(count - 1)])
    after = lax.ppermute(up_edge, axis, [(i + 1, i) for i in range(count - 1)])
    return before, after


def grid_rows(rows, halo, own):
    row = lax.axis_index("space") * own - halo + jnp.arange(rows)
    total = own * lax.axis_size("space")
    return ((row >= 0) & (row < total)).astype(jnp.float32)[None, :, None]


def stiffness_rows(field):
    padded = jnp.pad(field[:, 1:-1, :], ((0, 0), (0, 0), (1, 1)))
    neighbours = field[:, 2:, :] + field[:, :-2, :] + padded[:, :, 2:] + padded[:, :, :-2]
    return (kappa_square + 4.0) * field[:, 1:-1, :] - neighbours


def smooth(field, halo, own):
    once = stiffness_rows(field)
    once = once * grid_rows(once.shape[1], halo - 1, own)
    twice = stiffness_rows(once)
    if halo > 2:
        twice = twice * grid_rows(twice.shape[1], halo - 2, own)
    return twice


def recentre(sets, axis):
    count = lax.axis_size(axis)
    got = lax.all_to_all(jnp.broadcast_to(sets[None], (count,) + sets.shape), axis, 0, 0)
    uu, uw, ww, uy, wy, ratio = (got[:, k] for k in range(6))
    total = jnp.sum(uu, axis=0)
    centre = jnp.sum(uw + ratio * uu, axis=0) / total
    centre = jnp.where(total > 0, centre, 0.0)
    e = ratio - centre[None]
    ec = e * ratio
    uw_new = uw + e * uu
    ww_new = ww + e * (2.0 * uw + e * uu)
    uy_new = uy + e * uw + ec * uu
    wy_new = wy + e * (ww + ratio * uw + uy) + e * e * (uw + ratio * uu)
    parts = [total] + [jnp.sum(v, axis=0) for v in (uw_new, ww_new, uy_new, wy_new)] + [centre]
    return jnp.stack(parts + [jnp.zeros_like(total)] * 2)


def body(latent, counts, exposure, region_ids, coefficients):
    days, own, columns = latent.shape
    blocks = region_ids.shape[0]
    one_hot = (region_ids[:, None] == jnp.arange(coefficients.shape[0])[None, :]).astype(
        jnp.float32
    )
    block_offset = jnp.sum(one_hot * coefficients[None, :], axis=1)
    offset = jnp.broadcast_to(block_offset[:, None], (blocks, own // blocks)).reshape(own)
    intensity = exposure * jnp.exp(offset[None, :, None] + latent)
    excess = intensity - counts.astype(jnp.float32)

    def packed(lo):
        pieces = []
        for field, width in ((latent, 6), (excess, 4), (intensity, 2)):
            rows = field[:, :width] if lo else field[:, own - width :]
            pieces.append(rows.reshape(days * width, columns))
        return jnp.concatenate(pieces)

    above, below = exchange(packed(True), packed(False), "space")

    def unpacked(message):
        cut = (days * 6, days * 10)
        return (
            message[: cut[0]].reshape(days, 6, columns),
            message[cut[0] : cut[1]].reshape(days, 4, columns),
            message[cut[1] :].reshape(days, 2, columns),
        )

    latent6, excess4, intensity2 = (
        jnp.concatenate([a, field, b], axis=1)
        for a, field, b in zip(unpacked(above), (latent, excess, intensity), unpacked(below))
    )

    tm_at, tm_count = lax.axis_index("tm"), lax.axis_size("tm")
    has_before = (tm_at > 0).astype(jnp.float32)
    has_after = (tm_at < tm_count - 1).astype(jnp.float32)
    first = jnp.where(tm_at == 0, prior_scale, INNER).astype(jnp.float32)
    last = jnp.where(tm_at == tm_count - 1, prior_scale, INNER).astype(jnp.float32)
    weight = [first] + [jnp.float32(INNER)] * (days - 2) + [last]

    spatial = smooth(latent6, 6, own)
    on4 = grid_rows(own + 8, 4, own)[0]
    residual = []
    for t in range(days):
        value = weight[t] * spatial[t] + excess4[t]
        if t > 0:
            value = value - COUPLE * spatial[t - 1]
        if t < days - 1:
            value = value - COUPLE * spatial[t + 1]
        residual.append(-value * on4)
    inner = smooth(jnp.stack(residual[1:-1]), 4, own)
    to_before = jnp.concatenate([spatial[0], residual[0], -COUPLE * inner[0], intensity2[0]])
    to_after = jnp.concatenate([spatial[-1], residual[-1], -COUPLE * inner[-1], intensity2[-1]])
    from_before, from_after = exchange(to_before, to_after, "tm")

    def parts(message):
        a, b, c = own + 8, 2 * own + 16, 3 * own + 20
        return message[:a], message[a:b], message[b:c], message[c:]

    s_b, r_b, q_b, i_b = parts(from_before)
    s_a, r_a, q_a, i_a = parts(from_after)
    r_b = (r_b + COUPLE * spatial[0]) * has_before
    r_a = (r_a + COUPLE * spatial[-1]) * has_after
    residual[0] = residual[0] + COUPLE * s_b
    residual[-1] = residual[-1] + COUPLE * s_a
    outer = smooth(jnp.stack([r_b, residual[0], residual[-1], r_a]), 4, own)
    filtered = [outer[0], outer[1]] + [inner[k] for k in range(days - 2)] + [outer[2], outer[3]]
    mid = slice(2, -2)
    image = []
    for t in range(days):
        image.append(
            weight[t] * filtered[t + 1]
            - COUPLE * (filtered[t] + filtered[t + 2])
            + intensity2[t] * residual[t][mid]
        )
    image_b = (INNER * filtered[0] - COUPLE * filtered[1] + q_b + i_b * r_b[mid]) * has_before
    image_a = (INNER * filtered[-1] - COUPLE * filtered[-2] + q_a + i_a * r_a[mid]) * has_after
    twice = smooth(jnp.stack([image_b] + image + [image_a]), 2, own)
    u = jnp.stack([value[4:-4] for value in residual])
    q = jnp.stack([value[mid] for value in image])
    z = jnp.stack(
        [
            weight[t] * twice[t + 1]
            - COUPLE * (twice[t] + twice[t + 2])
            + intensity[t] * q[t]
            for t in range(days)
        ]
    )

    uu, uq = jnp.sum(u * u), jnp.sum(u * q)
    ratio = jnp.where(uu > 0, uq / uu, 0.0)
    w = q - ratio * u
    y = z - ratio * q
    moments = jnp.stack(
        [uu, jnp.sum(u * w), jnp.sum(w * w), jnp.sum(u * y), jnp.sum(w * y), ratio, uu, uu]
    )
    sets = jnp.broadcast_to(moments[:, None], (8, 128))
    sets = recentre(recentre(sets, "tm"), "space")
    m0, ww, wy, centre = sets[0, 0], sets[2, 0], sets[4, 0], sets[5, 0]
    alpha0 = 1.0 / centre
    norm1 = alpha0 * alpha0 * ww
    beta = norm1 / m0
    curvature1 = alpha0 * alpha0 * wy - beta * beta * (centre * m0)
    alpha1 = norm1 / curvature1
    residual1 = u - alpha0 * q
    direction1 = residual1 + beta * u
    image1 = (q - alpha0 * z) + beta * q
    return (latent + (alpha0 * u + alpha1 * direction1), residual1 - alpha1 * image1)


def solution(mesh):
    return jax.shard_map(
        body,
        mesh=mesh,
        in_specs=(
            P("tm", "space", None),
            P("tm", "space", None),
            P("tm", "space", None),
            P("space"),
            P(),
        ),
        out_specs=(P("tm", "space", None), P("tm", "space", None)),
        check_vma=False,
    )
```

```python
import functools

import jax
import jax.numpy as jnp
from jax import lax
from jax.experimental import pallas as pl
from jax.experimental.pallas import tpu as pltpu
from jax.sharding import PartitionSpec as P

kappa_square = 0.3
time_corr = 0.9
prior_scale = 0.05

COUPLE = prior_scale * time_corr
INNER = prior_scale * (1.0 + time_corr * time_corr)
DIAG = kappa_square + 4.0

DAYS, OWN, COLUMNS = 4, 32, 1024
PAD = 8
FRAME = OWN + 2 * PAD
TILES = FRAME // 8
REGION_ROWS = 4
WIDE, SLIM = OWN + 8, OWN + 4
MESSAGE = 2 * WIDE + 2 * SLIM
EDGE = DAYS * 12

VMEM = pl.BlockSpec(memory_space=pltpu.VMEM)
SMEM = pl.BlockSpec(memory_space=pltpu.SMEM)
PARAMS = pltpu.CompilerParams(vmem_limit_bytes=40 * 1024 * 1024)


def f32(*shape):
    return jax.ShapeDtypeStruct(shape, jnp.float32)


def row_iota():
    return lax.broadcasted_iota(jnp.int32, (8, COLUMNS), 0)


def column_iota():
    return lax.broadcasted_iota(jnp.int32, (8, COLUMNS), 1)


def tile(i):
    return pl.ds(pl.multiple_of(i * 8, 8), 8)


def on_grid(at_ref, i):
    sp, count = at_ref[0], at_ref[2]
    off = ((i == 0) & (sp == 0)) | ((i == TILES - 1) & (sp == count - 1))
    return jnp.logical_not(off)


def apply_k(at_ref, src, dst, planes):
    row, column = row_iota(), column_iota()

    def step(i, carry):
        keep = on_grid(at_ref, i)
        for s, d in planes:
            cur = src[s, tile(i), :]
            prev = src[s, tile(jnp.maximum(i - 1, 0)), :]
            nxt = src[s, tile(jnp.minimum(i + 1, TILES - 1)), :]
            up = pltpu.roll(jnp.where(row == 7, prev, cur), 1, 0)
            down = pltpu.roll(jnp.where(row == 0, nxt, cur), 7, 0)
            left = jnp.where(column == 0, 0.0, pltpu.roll(cur, 1, 1))
            right = jnp.where(column == COLUMNS - 1, 0.0, pltpu.roll(cur, COLUMNS - 1, 1))
            out = DIAG * cur - ((up + down) + (left + right))
            dst[d, tile(i), :] = jnp.where(keep, out, 0.0)
        return carry

    lax.fori_loop(0, TILES, step, 0)


def day_weights(at_ref):
    tm, count = at_ref[1], at_ref[3]
    first = jnp.where(tm == 0, prior_scale, INNER).astype(jnp.float32)
    last = jnp.where(tm == count - 1, prior_scale, INNER).astype(jnp.float32)
    return [first] + [jnp.float32(INNER)] * (DAYS - 2) + [last]


def intensity_kernel(ids, coef, latent, counts, exposure, intensity, excess, head, tail):
    row = row_iota()
    for i in range(OWN // 8):
        rows = slice(8 * i, 8 * i + 8)
        offset = jnp.where(row < REGION_ROWS, coef[ids[2 * i]], coef[ids[2 * i + 1]])
        for t in range(DAYS):
            value = exposure[t, rows, :] * jnp.exp(offset + latent[t, rows, :])
            intensity[t, rows, :] = value
            excess[t, rows, :] = value - counts[t, rows, :].astype(jnp.float32)
    start = 0
    for field, width in ((latent, 6), (excess, 4), (intensity, 2)):
        for t in range(DAYS):
            head[start : start + width, :] = field[t, :width, :]
            tail[start : start + width, :] = field[t, OWN - width :, :]
            start += width


def residual_kernel(
    at, latent, excess, intensity, above, below, res, inten, ends, inner, y_msg, c_msg, lat, exc, tmp
):
    start = 0
    for field, frame, width in ((latent, lat, 6), (excess, exc, 4), (intensity, inten, 2)):
        for t in range(DAYS):
            frame[t, PAD : PAD + OWN, :] = field[t]
            frame[t, PAD - width : PAD, :] = above[start : start + width, :]
            frame[t, PAD + OWN : PAD + OWN + width, :] = below[start : start + width, :]
            start += width
    same = [(t, t) for t in range(DAYS)]
    apply_k(at, lat, tmp, same)
    apply_k(at, tmp, lat, same)
    weight = day_weights(at)

    def combine(i, carry):
        s = [lat[t, tile(i), :] for t in range(DAYS)]
        for t in range(DAYS):
            value = weight[t] * s[t] + exc[t, tile(i), :]
            if t > 0:
                value = value - COUPLE * s[t - 1]
            if t < DAYS - 1:
                value = value - COUPLE * s[t + 1]
            res[t, tile(i), :] = -value
        ends[0, tile(i), :] = s[0]
        ends[1, tile(i), :] = s[DAYS - 1]
        return carry

    lax.fori_loop(0, TILES, combine, 0)
    middle = list(range(DAYS - 2))
    apply_k(at, res, tmp, [(k + 1, k) for k in middle])
    apply_k(at, tmp, inner, [(k, k) for k in middle])

    def pack(msg, day, nearest):
        msg[:WIDE, :] = lat[day, PAD - 4 : PAD + OWN + 4, :]
        msg[WIDE : 2 * WIDE, :] = res[day, PAD - 4 : PAD + OWN + 4, :]
        msg[2 * WIDE : 2 * WIDE + SLIM, :] = -COUPLE * inner[nearest, PAD - 2 : PAD + OWN + 2, :]
        msg[2 * WIDE + SLIM :, :] = inten[day, PAD - 2 : PAD + OWN + 2, :]

    even = lax.rem(at[1], 2) == 0

    @pl.when(even)
    def _():
        pack(y_msg, 0, 0)
        pack(c_msg, DAYS - 1, DAYS - 3)

    @pl.when(jnp.logical_not(even))
    def _():
        pack(c_msg, 0, 0)
        pack(y_msg, DAYS - 1, DAYS - 3)


def image_kernel(
    at, res, inten, ends, inner, intensity, y_msg, c_msg, u_out, q_out, z_out, sets, r6, f6, q6, tmp, got
):
    even = lax.rem(at[1], 2) == 0

    def unpack(msg, side):
        got[side, PAD - 4 : PAD + OWN + 4, :] = msg[:WIDE, :]
        got[2 + side, PAD - 4 : PAD + OWN + 4, :] = msg[WIDE : 2 * WIDE, :]
        got[4 + side, PAD - 2 : PAD + OWN + 2, :] = msg[2 * WIDE : 2 * WIDE + SLIM, :]
        got[6 + side, PAD - 2 : PAD + OWN + 2, :] = msg[2 * WIDE + SLIM :, :]

    @pl.when(even)
    def _():
        unpack(y_msg, 0)
        unpack(c_msg, 1)

    @pl.when(jnp.logical_not(even))
    def _():
        unpack(c_msg, 0)
        unpack(y_msg, 1)

    has = (at[1] > 0, at[1] < at[3] - 1)
    weight = day_weights(at)
    last = DAYS + 1

    def finish(i, carry):
        r6[0, tile(i), :] = jnp.where(has[0], got[2, tile(i), :] + COUPLE * ends[0, tile(i), :], 0.0)
        r6[last, tile(i), :] = jnp.where(has[1], got[3, tile(i), :] + COUPLE * ends[1, tile(i), :], 0.0)
        r6[1, tile(i), :] = res[0, tile(i), :] + COUPLE * got[0, tile(i), :]
        r6[DAYS, tile(i), :] = res[DAYS - 1, tile(i), :] + COUPLE * got[1, tile(i), :]
        for t in range(1, DAYS - 1):
            r6[t + 1, tile(i), :] = res[t, tile(i), :]
            f6[t + 1, tile(i), :] = inner[t - 1, tile(i), :]
        return carry

    lax.fori_loop(0, TILES, finish, 0)
    outer = [(0, 0), (1, 1), (DAYS, DAYS), (last, last)]
    apply_k(at, r6, tmp, outer)
    apply_k(at, tmp, f6, outer)

    def image(i, carry):
        f = [f6[t, tile(i), :] for t in range(DAYS + 2)]
        r = [r6[t, tile(i), :] for t in range(DAYS + 2)]
        for t in range(DAYS):
            q6[t + 1, tile(i), :] = (
                weight[t] * f[t + 1] - COUPLE * (f[t] + f[t + 2]) + inten[t, tile(i), :] * r[t + 1]
            )
        before = INNER * f[0] - COUPLE * f[1] + got[4, tile(i), :] + got[6, tile(i), :] * r[0]
        after = INNER * f[last] - COUPLE * f[DAYS] + got[5, tile(i), :] + got[7, tile(i), :] * r[last]
        q6[0, tile(i), :] = jnp.where(has[0], before, 0.0)
        q6[last, tile(i), :] = jnp.where(has[1], after, 0.0)
        return carry

    lax.fori_loop(0, TILES, image, 0)
    every = [(t, t) for t in range(DAYS + 2)]
    apply_k(at, q6, tmp, every)
    apply_k(at, tmp, f6, every)
    zero = jnp.zeros((8, COLUMNS), jnp.float32)

    def product(i, carry):
        uu, uq = carry
        k = i + PAD // 8
        f = [f6[t, tile(k), :] for t in range(DAYS + 2)]
        for t in range(DAYS):
            q, u = q6[t + 1, tile(k), :], r6[t + 1, tile(k), :]
            z = weight[t] * f[t + 1] - COUPLE * (f[t] + f[t + 2]) + intensity[t, tile(i), :] * q
            z_out[t, tile(i), :] = z
            q_out[t, tile(i), :] = q
            u_out[t, tile(i), :] = u
            uu = uu + u * u
            uq = uq + u * q
        return uu, uq

    uu, uq = lax.fori_loop(0, OWN // 8, product, (zero, zero))

    def total(v):
        return jnp.sum(jnp.sum(v, axis=0, keepdims=True), axis=1, keepdims=True)

    uu, uq = total(uu), total(uq)
    ratio = jnp.where(uu > 0, uq / uu, 0.0)

    def moment(i, carry):
        uw, ww, uy, wy = carry
        for t in range(DAYS):
            u, q, z = u_out[t, tile(i), :], q_out[t, tile(i), :], z_out[t, tile(i), :]
            w = q - ratio * u
            y = z - ratio * q
            uw, ww, uy, wy = uw + u * w, ww + w * w, uy + u * y, wy + w * y
        return uw, ww, uy, wy

    rest = [total(v) for v in lax.fori_loop(0, OWN // 8, moment, (zero,) * 4)]
    write_sets(sets, [uu] + rest + [ratio])


def write_sets(sets, values):
    row = lax.broadcasted_iota(jnp.int32, (8, 128), 0)
    out = jnp.zeros((8, 128), jnp.float32)
    for k, value in enumerate(values):
        out = jnp.where(row == k, value, out)
    for n in range(sets.shape[0]):
        sets[n] = out


def recentred(got):
    uu, uw, ww, uy, wy, ratio = (got[:, k, :] for k in range(6))

    def add(v):
        return jnp.sum(v, axis=0, keepdims=True)

    total = add(uu)
    centre = jnp.where(total > 0, add(uw + ratio * uu) / total, 0.0)
    e = ratio - centre
    uw_new = uw + e * uu
    ww_new = ww + e * (2.0 * uw + e * uu)
    uy_new = uy + e * uw + e * ratio * uu
    wy_new = wy + e * (ww + ratio * uw + uy) + e * e * (uw + ratio * uu)
    return total, add(uw_new), add(ww_new), add(uy_new), add(wy_new), centre


def regroup_kernel(got, sets):
    write_sets(sets, recentred(got))


def update_kernel(got, latent, u_in, q_in, z_in, updated, residual):
    m0, _, ww, _, wy, centre = (v[:, :1] for v in recentred(got))
    alpha0 = 1.0 / centre
    norm1 = alpha0 * alpha0 * ww
    beta = norm1 / m0
    curvature1 = alpha0 * alpha0 * wy - beta * beta * (centre * m0)
    alpha1 = norm1 / curvature1
    for i in range(OWN // 8):
        rows = slice(8 * i, 8 * i + 8)
        u, q, z = u_in[0, rows, :], q_in[0, rows, :], z_in[0, rows, :]
        residual1 = u - alpha0 * q
        direction1 = residual1 + beta * u
        image1 = (q - alpha0 * z) + beta * q
        updated[0, rows, :] = latent[0, rows, :] + (alpha0 * u + alpha1 * direction1)
        residual[0, rows, :] = residual1 - alpha1 * image1


def gathered(sets, axis):
    return lax.all_to_all(sets, axis, 0, 0)


def body(latent, counts, exposure, region_ids, coefficients):
    field = f32(DAYS, OWN, COLUMNS)
    spaces, times = lax.axis_size("space"), lax.axis_size("tm")
    at = jnp.stack(
        [lax.axis_index("space"), lax.axis_index("tm"), jnp.int32(spaces), jnp.int32(times)]
    ).astype(jnp.int32)

    intensity, excess, head, tail = pl.pallas_call(
        intensity_kernel,
        out_shape=(field, field, f32(EDGE, COLUMNS), f32(EDGE, COLUMNS)),
        in_specs=[SMEM, SMEM, VMEM, VMEM, VMEM],
        out_specs=(VMEM,) * 4,
        compiler_params=PARAMS,
        name="intensity",
    )(region_ids, coefficients, latent, counts, exposure)

    above = lax.ppermute(tail, "space", [(i, i + 1) for i in range(spaces - 1)])
    below = lax.ppermute(head, "space", [(i + 1, i) for i in range(spaces - 1)])

    frames = functools.partial(f32, FRAME, COLUMNS)
    res, inten, ends, inner, y_msg, c_msg = pl.pallas_call(
        residual_kernel,
        out_shape=(
            f32(DAYS, FRAME, COLUMNS),
            f32(DAYS, FRAME, COLUMNS),
            f32(2, FRAME, COLUMNS),
            f32(DAYS - 2, FRAME, COLUMNS),
            f32(MESSAGE, COLUMNS),
            f32(MESSAGE, COLUMNS),
        ),
        in_specs=[SMEM] + [VMEM] * 5,
        out_specs=(VMEM,) * 6,
        scratch_shapes=[pltpu.VMEM((DAYS, FRAME, COLUMNS), jnp.float32)] * 3,
        compiler_params=PARAMS,
        name="residual",
    )(at, latent, excess, intensity, above, below)

    across = [p for i in range(1, times - 1, 2) for p in ((i, i + 1), (i + 1, i))]
    within = [p for i in range(0, times - 1, 2) for p in ((i, i + 1), (i + 1, i))]
    y_got = lax.ppermute(y_msg, "tm", across)
    c_got = lax.ppermute(c_msg, "tm", within)

    six = pltpu.VMEM((DAYS + 2, FRAME, COLUMNS), jnp.float32)
    u, q, z, sets = pl.pallas_call(
        image_kernel,
        out_shape=(field, field, field, f32(times, 8, 128)),
        in_specs=[SMEM] + [VMEM] * 7,
        out_specs=(VMEM,) * 4,
        scratch_shapes=[six] * 4 + [pltpu.VMEM((8, FRAME, COLUMNS), jnp.float32)],
        compiler_params=PARAMS,
        name="image",
    )(at, res, inten, ends, inner, intensity, y_got, c_got)

    sets = pl.pallas_call(
        regroup_kernel,
        out_shape=f32(spaces, 8, 128),
        in_specs=[VMEM],
        out_specs=VMEM,
        name="regroup",
    )(gathered(sets, "tm"))

    day = pl.BlockSpec((1, OWN, COLUMNS), lambda t: (t, 0, 0))
    return pl.pallas_call(
        update_kernel,
        grid=(DAYS,),
        out_shape=(field, field),
        in_specs=[pl.BlockSpec((spaces, 8, 128), lambda t: (0, 0, 0))] + [day] * 4,
        out_specs=(day, day),
        compiler_params=PARAMS,
        name="update",
    )(gathered(sets, "space"), latent, u, q, z)


def solution(mesh):
    return jax.shard_map(
        body,
        mesh=mesh,
        in_specs=(
            P("tm", "space", None),
            P("tm", "space", None),
            P("tm", "space", None),
            P("space"),
            P(),
        ),
        out_specs=(P("tm", "space", None), P("tm", "space", None)),
        check_vma=False,
    )
```

```python
import functools

import jax
import jax.numpy as jnp
from jax import lax
from jax.experimental import pallas as pl
from jax.experimental.pallas import tpu as pltpu
from jax.sharding import PartitionSpec as P

kappa_square = 0.3
time_corr = 0.9
prior_scale = 0.05

COUPLE = prior_scale * time_corr
INNER = prior_scale * (1.0 + time_corr * time_corr)
DIAG = kappa_square + 4.0

DAYS, OWN, COLUMNS = 4, 32, 1024
TILES = OWN // 8 + 2
FRAME = 8 * TILES
BOTTOM = TILES - 1
OWN_TILES = range(1, BOTTOM)
REGION_ROWS = 4
EDGE = 8 * (DAYS + DAYS // 2)
MESSAGE_TILES = 2 * (OWN // 8 + 1) + 2 * (OWN // 8) + 1
S_AT, R_AT, Q_AT, I_AT, H_AT = 0, 5, 10, 14, 18

VMEM = pl.BlockSpec(memory_space=pltpu.VMEM)
HBM = pl.BlockSpec(memory_space=pltpu.HBM)
PARAMS = pltpu.CompilerParams(vmem_limit_bytes=40 * 1024 * 1024)


def f32(*shape):
    return jax.ShapeDtypeStruct(shape, jnp.float32)


def rows(i):
    return slice(8 * i, 8 * i + 8)


def row_iota():
    return lax.broadcasted_iota(jnp.int32, (8, COLUMNS), 0)


def up_roll(v, k):
    return pltpu.roll(v, k, 0)


def places():
    sp, tm = lax.axis_index("space"), lax.axis_index("tm")
    spaces, times = lax.axis_size("space"), lax.axis_size("tm")
    return sp > 0, sp < spaces - 1, tm > 0, tm < times - 1, lax.rem(tm, 2) == 0


def framed(ref):
    return lambda s, i: ref[s, rows(i), :]


def apply_k(load, dst, planes, has_above, has_below, tiles=range(TILES)):
    row = row_iota()
    lane = lax.broadcasted_iota(jnp.int32, (8, 128), 1)
    for s, d in planes:
        cur = load(s, tiles[0])
        prev = load(s, tiles[0] - 1) if tiles[0] > 0 else cur
        for i in tiles:
            nxt = load(s, i + 1) if i < BOTTOM else cur
            up = up_roll(jnp.where(row == 7, prev, cur), 1)
            down = up_roll(jnp.where(row == 0, nxt, cur), 7)
            left = pltpu.roll(cur, 1, 1)
            right = pltpu.roll(cur, COLUMNS - 1, 1)
            left = jnp.concatenate([jnp.where(lane == 0, 0.0, left[:, :128]), left[:, 128:]], axis=1)
            right = jnp.concatenate(
                [right[:, :-128], jnp.where(lane == 127, 0.0, right[:, -128:])], axis=1
            )
            out = DIAG * cur - ((up + down) + (left + right))
            if i == 0:
                out = jnp.where(has_above, out, 0.0)
            if i == BOTTOM:
                out = jnp.where(has_below, out, 0.0)
            dst[d, rows(i), :] = out
            prev, cur = cur, nxt


def day_weights(has_before, has_after):
    first = jnp.where(has_before, INNER, prior_scale).astype(jnp.float32)
    last = jnp.where(has_after, INNER, prior_scale).astype(jnp.float32)
    return [first] + [jnp.float32(INNER)] * (DAYS - 2) + [last]


def intensity_kernel(
    ids_in, coef_in, latent, counts, exposure, lat, exc, inten, head, tail, ids, coef, cnt, exposed, sems
):
    small = [
        pltpu.make_async_copy(ids_in, ids, sems.at[3 * DAYS]),
        pltpu.make_async_copy(coef_in, coef, sems.at[3 * DAYS + 1]),
    ]
    days = [
        (
            pltpu.make_async_copy(latent.at[t], lat.at[t], sems.at[3 * t]),
            pltpu.make_async_copy(exposure.at[t], exposed.at[t], sems.at[3 * t + 1]),
            pltpu.make_async_copy(counts.at[t], cnt.at[t], sems.at[3 * t + 2]),
        )
        for t in range(DAYS)
    ]
    for copy in small:
        copy.start()
    for copies in days:
        for copy in copies:
            copy.start()
    for copy in small:
        copy.wait()
    row = row_iota()
    blocks = 8 // REGION_ROWS
    offsets = [
        jnp.where(row < REGION_ROWS, coef[ids[blocks * i]], coef[ids[blocks * i + 1]])
        for i in range(OWN // 8)
    ]
    for t in range(DAYS):
        for copy in days[t]:
            copy.wait()
        for i in range(OWN // 8):
            value = exposed[t, rows(i), :] * jnp.exp(offsets[i] + lat[t, rows(i), :])
            inten[t, rows(i), :] = value
            exc[t, rows(i), :] = value - cnt[t, rows(i), :].astype(jnp.float32)
    last = OWN // 8 - 1
    for t in range(DAYS):
        tail[rows(t), :] = jnp.where(row < 2, up_roll(inten[t, rows(last), :], 2), lat[t, rows(last), :])
        head[rows(t), :] = jnp.where(row >= 6, up_roll(inten[t, rows(0), :], 6), lat[t, rows(0), :])
    for k in range(DAYS // 2):
        a, b = 2 * k, 2 * k + 1
        tail[rows(DAYS + k), :] = jnp.where(
            row >= 4, exc[a, rows(last), :], up_roll(exc[b, rows(last), :], 4)
        )
        head[rows(DAYS + k), :] = jnp.where(row < 4, exc[a, rows(0), :], up_roll(exc[b, rows(0), :], 4))


def residual_kernel(latent, inten, exc, above, below, lat, res, inner, y_msg, c_msg, tmp):
    has_above, has_below, has_before, has_after, even = places()
    row = row_iota()

    def field(t, i):
        if i in OWN_TILES:
            return latent[t, rows(i - 1), :]
        return (above if i == 0 else below)[rows(t), :]

    same = [(t, t) for t in range(DAYS)]
    apply_k(field, tmp, same, has_above, has_below)
    apply_k(framed(tmp), lat, same, has_above, has_below)
    weight = day_weights(has_before, has_after)

    for i in range(TILES):
        s = [lat[t, rows(i), :] for t in range(DAYS)]
        for t in range(DAYS):
            if i in (0, BOTTOM):
                excess = (above if i == 0 else below)[rows(DAYS + t // 2), :]
                excess = up_roll(excess, 4) if t % 2 else excess
            else:
                excess = exc[t, rows(i - 1), :]
            value = weight[t] * s[t] + excess
            if t > 0:
                value = value - COUPLE * s[t - 1]
            if t < DAYS - 1:
                value = value - COUPLE * s[t + 1]
            res[t, rows(i), :] = -value
    middle = range(DAYS - 2)
    apply_k(framed(res), tmp, [(k + 1, k) for k in middle], has_above, has_below)
    apply_k(framed(tmp), inner, [(k, k) for k in middle], has_above, has_below)

    def send(at, before, after):
        y_msg[rows(at), :] = jnp.where(even, before, after)
        c_msg[rows(at), :] = jnp.where(even, after, before)

    def halo(field, day):
        return jnp.where(row < 4, field[day, rows(BOTTOM), :], field[day, rows(0), :])

    first, last = 0, DAYS - 1
    for i in OWN_TILES:
        send(S_AT + i, lat[first, rows(i), :], lat[last, rows(i), :])
        send(R_AT + i, res[first, rows(i), :], res[last, rows(i), :])
        send(Q_AT + i - 1, -COUPLE * inner[0, rows(i), :], -COUPLE * inner[DAYS - 3, rows(i), :])
        send(I_AT + i - 1, inten[first, rows(i - 1), :], inten[last, rows(i - 1), :])
    send(S_AT, halo(lat, first), halo(lat, last))
    send(R_AT, halo(res, first), halo(res, last))
    outer = (row < 2) | (row >= 6)

    def slim(day, near):
        wanted = jnp.where(row < 4, up_roll(above[rows(day), :], 2), up_roll(below[rows(day), :], 6))
        return jnp.where(outer, -COUPLE * halo(inner, near), wanted)

    send(H_AT, slim(first, 0), slim(last, DAYS - 3))


def image_kernel(
    res, inner, lat, inten, above, below, y_msg, c_msg, u_out, q_out, z_out, sets, r6, q6, f6, tmp
):
    has_above, has_below, has_before, has_after, even = places()
    weight = day_weights(has_before, has_after)
    last = DAYS + 1

    def got(at):
        y, c = y_msg[rows(at), :], c_msg[rows(at), :]
        return jnp.where(even, y, c), jnp.where(even, c, y)

    for i in range(TILES):
        k = i if i in OWN_TILES else 0
        s_before, s_after = got(S_AT + k)
        r_before, r_after = got(R_AT + k)
        r6[0, rows(i), :] = jnp.where(has_before, r_before + COUPLE * lat[0, rows(i), :], 0.0)
        r6[last, rows(i), :] = jnp.where(has_after, r_after + COUPLE * lat[DAYS - 1, rows(i), :], 0.0)
        r6[1, rows(i), :] = res[0, rows(i), :] + COUPLE * s_before
        r6[DAYS, rows(i), :] = res[DAYS - 1, rows(i), :] + COUPLE * s_after
    outer = [(0, 0), (1, 1), (DAYS, DAYS), (last, last)]
    apply_k(framed(r6), tmp, outer, has_above, has_below)
    apply_k(framed(tmp), f6, outer, has_above, has_below)

    def residual(t, i):
        return r6[t, rows(i), :] if (t, t) in outer else res[t - 1, rows(i), :]

    def intensity(t, i):
        if i in OWN_TILES:
            return inten[t, rows(i - 1), :]
        return up_roll(above[rows(t), :], 6) if i == 0 else up_roll(below[rows(t), :], 2)

    for i in range(TILES):
        f = [
            f6[t, rows(i), :] if (t, t) in outer else inner[t - 2, rows(i), :]
            for t in range(DAYS + 2)
        ]
        r = [residual(t, i) for t in range(DAYS + 2)]
        for t in range(DAYS):
            q6[t + 1, rows(i), :] = (
                weight[t] * f[t + 1] - COUPLE * (f[t] + f[t + 2]) + intensity(t, i) * r[t + 1]
            )
        if i in OWN_TILES:
            q_side, i_side = got(Q_AT + i - 1), got(I_AT + i - 1)
        else:
            q_side = got(H_AT)
            i_side = [up_roll(v, 4) for v in q_side]
        before = INNER * f[0] - COUPLE * f[1] + q_side[0] + i_side[0] * r[0]
        after = INNER * f[last] - COUPLE * f[DAYS] + q_side[1] + i_side[1] * r[last]
        q6[0, rows(i), :] = jnp.where(has_before, before, 0.0)
        q6[last, rows(i), :] = jnp.where(has_after, after, 0.0)
    every = [(t, t) for t in range(DAYS + 2)]
    apply_k(framed(q6), tmp, every, has_above, has_below)
    apply_k(framed(tmp), f6, every, has_above, has_below, OWN_TILES)
    zero = jnp.zeros((8, COLUMNS), jnp.float32)

    uu = uq = zero
    for i in OWN_TILES:
        f = [f6[t, rows(i), :] for t in range(DAYS + 2)]
        for t in range(DAYS):
            q, u = q6[t + 1, rows(i), :], residual(t + 1, i)
            z = weight[t] * f[t + 1] - COUPLE * (f[t] + f[t + 2]) + intensity(t, i) * q
            z_out[t, rows(i - 1), :] = z
            q_out[t, rows(i - 1), :] = q
            u_out[t, rows(i - 1), :] = u
            uu = uu + u * u
            uq = uq + u * q

    def total(v):
        return jnp.sum(jnp.sum(v, axis=0, keepdims=True), axis=1, keepdims=True)

    uu, uq = total(uu), total(uq)
    ratio = jnp.where(uu > 0, uq / uu, 0.0)
    uw = ww = uy = wy = zero
    for i in range(OWN // 8):
        for t in range(DAYS):
            u, q, z = u_out[t, rows(i), :], q_out[t, rows(i), :], z_out[t, rows(i), :]
            w = q - ratio * u
            y = z - ratio * q
            uw, ww, uy, wy = uw + u * w, ww + w * w, uy + u * y, wy + w * y
    write_sets(sets, [uu, total(uw), total(ww), total(uy), total(wy), ratio])


def write_sets(sets, values):
    row = lax.broadcasted_iota(jnp.int32, (8, 128), 0)
    out = jnp.zeros((8, 128), jnp.float32)
    for k, value in enumerate(values):
        out = jnp.where(row == k, value, out)
    for n in range(sets.shape[0] // 8):
        sets[rows(n), :] = out


def recentred(got):
    senders = got.shape[0] // 8
    uu, uw, ww, uy, wy, ratio = (got[pl.ds(k, senders, 8), :] for k in range(6))

    def add(v):
        return jnp.sum(v, axis=0, keepdims=True)

    total = add(uu)
    centre = jnp.where(total > 0, add(uw + ratio * uu) / total, 0.0)
    e = ratio - centre
    uw_new = uw + e * uu
    ww_new = ww + e * (2.0 * uw + e * uu)
    uy_new = uy + e * uw + e * ratio * uu
    wy_new = wy + e * (ww + ratio * uw + uy) + e * e * (uw + ratio * uu)
    return total, add(uw_new), add(ww_new), add(uy_new), add(wy_new), centre


def regroup_kernel(got, sets):
    write_sets(sets, recentred(got))


def update_kernel(got, latent, u_in, q_in, z_in, updated, residual, factors):
    @pl.when(pl.program_id(0) == 0)
    def _():
        m0, _, ww, _, wy, centre = recentred(got)
        alpha0 = 1.0 / centre
        norm1 = alpha0 * alpha0 * ww
        beta = norm1 / m0
        curvature1 = alpha0 * alpha0 * wy - beta * beta * (centre * m0)
        factors[0:1, :] = alpha0
        factors[1:2, :] = beta
        factors[2:3, :] = norm1 / curvature1

    alpha0, beta, alpha1 = (factors[k : k + 1, 0:1] for k in range(3))
    for i in range(OWN // 8):
        u, q, z = u_in[0, rows(i), :], q_in[0, rows(i), :], z_in[0, rows(i), :]
        residual1 = u - alpha0 * q
        direction1 = residual1 + beta * u
        image1 = (q - alpha0 * z) + beta * q
        updated[0, rows(i), :] = latent[0, rows(i), :] + (alpha0 * u + alpha1 * direction1)
        residual[0, rows(i), :] = residual1 - alpha1 * image1


def gathered(sets, axis):
    count = lax.axis_size(axis)
    got = lax.all_to_all(sets.reshape(count, 8, 128), axis, 0, 0)
    return got.reshape(8 * count, 128)


def body(latent, counts, exposure, region_ids, coefficients):
    spaces, times = lax.axis_size("space"), lax.axis_size("tm")
    field, four = f32(DAYS, OWN, COLUMNS), f32(DAYS, FRAME, COLUMNS)
    edge, message = f32(EDGE, COLUMNS), f32(8 * MESSAGE_TILES, COLUMNS)

    def vmem(shape, dtype=jnp.float32):
        return pltpu.VMEM(shape, dtype)

    lat, exc, inten, head, tail = pl.pallas_call(
        intensity_kernel,
        out_shape=(field, field, field, edge, edge),
        in_specs=[HBM] * 5,
        out_specs=(VMEM,) * 5,
        scratch_shapes=[
            pltpu.SMEM(region_ids.shape, jnp.int32),
            pltpu.SMEM(coefficients.shape, jnp.float32),
            vmem(counts.shape, jnp.int32),
            vmem(exposure.shape),
            pltpu.SemaphoreType.DMA((3 * DAYS + 2,)),
        ],
        compiler_params=PARAMS,
        name="intensity",
    )(region_ids, coefficients, latent, counts, exposure)

    above = lax.ppermute(tail, "space", [(i, i + 1) for i in range(spaces - 1)])
    below = lax.ppermute(head, "space", [(i + 1, i) for i in range(spaces - 1)])

    spatial, res, inner, y_msg, c_msg = pl.pallas_call(
        residual_kernel,
        out_shape=(four, four, f32(DAYS - 2, FRAME, COLUMNS), message, message),
        in_specs=[VMEM] * 5,
        out_specs=(VMEM,) * 5,
        scratch_shapes=[vmem(four.shape)],
        compiler_params=PARAMS,
        name="residual",
    )(lat, inten, exc, above, below)

    across = [p for i in range(1, times - 1, 2) for p in ((i, i + 1), (i + 1, i))]
    within = [p for i in range(0, times - 1, 2) for p in ((i, i + 1), (i + 1, i))]
    y_got = lax.ppermute(y_msg, "tm", across)
    c_got = lax.ppermute(c_msg, "tm", within)

    six = vmem((DAYS + 2, FRAME, COLUMNS))
    u, q, z, sets = pl.pallas_call(
        image_kernel,
        out_shape=(field, field, field, f32(8 * times, 128)),
        in_specs=[VMEM] * 8,
        out_specs=(VMEM,) * 4,
        scratch_shapes=[six] * 4,
        compiler_params=PARAMS,
        name="image",
    )(res, inner, spatial, inten, above, below, y_got, c_got)

    sets = pl.pallas_call(
        regroup_kernel,
        out_shape=f32(8 * spaces, 128),
        in_specs=[VMEM],
        out_specs=VMEM,
        name="regroup",
    )(gathered(sets, "tm"))

    day = pl.BlockSpec((1, OWN, COLUMNS), lambda t: (t, 0, 0))
    return pl.pallas_call(
        update_kernel,
        grid=(DAYS,),
        out_shape=(field, field),
        in_specs=[pl.BlockSpec((8 * spaces, 128), lambda t: (0, 0)), day, day, day, day],
        out_specs=(day, day),
        scratch_shapes=[vmem((8, 128))],
        compiler_params=PARAMS,
        name="update",
    )(gathered(sets, "space"), latent, u, q, z)


def solution(mesh):
    return jax.shard_map(
        body,
        mesh=mesh,
        in_specs=(
            P("tm", "space", None),
            P("tm", "space", None),
            P("tm", "space", None),
            P("space"),
            P(),
        ),
        out_specs=(P("tm", "space", None), P("tm", "space", None)),
        check_vma=False,
    )
```

```python
import functools

import jax
import jax.numpy as jnp
from jax import lax
from jax.experimental import pallas as pl
from jax.experimental.pallas import tpu as pltpu
from jax.sharding import PartitionSpec as P

kappa_square = 0.3
time_corr = 0.9
prior_scale = 0.05

COUPLE = prior_scale * time_corr
INNER = prior_scale * (1.0 + time_corr * time_corr)
DIAG = kappa_square + 4.0

DAYS, OWN, COLUMNS = 4, 32, 1024
TILES = OWN // 8 + 2
FRAME = 8 * TILES
BOTTOM = TILES - 1
OWN_TILES = range(1, BOTTOM)
REGION_ROWS = 4
EDGE = 8 * (DAYS + DAYS // 2)
MESSAGE_TILES = 2 * (OWN // 8 + 1) + 2 * (OWN // 8) + 1
S_AT, R_AT, Q_AT, I_AT, H_AT = 0, 5, 10, 14, 18

VMEM = pl.BlockSpec(memory_space=pltpu.VMEM)
HBM = pl.BlockSpec(memory_space=pltpu.HBM)
PARAMS = pltpu.CompilerParams(vmem_limit_bytes=40 * 1024 * 1024)
FETCHING = pltpu.CompilerParams(vmem_limit_bytes=53000 * 1024)


def f32(*shape):
    return jax.ShapeDtypeStruct(shape, jnp.float32)


def rows(i):
    return slice(8 * i, 8 * i + 8)


def row_iota():
    return lax.broadcasted_iota(jnp.int32, (8, COLUMNS), 0)


def up_roll(v, k):
    return pltpu.roll(v, k, 0)


def places():
    sp, tm = lax.axis_index("space"), lax.axis_index("tm")
    spaces, times = lax.axis_size("space"), lax.axis_size("tm")
    return sp > 0, sp < spaces - 1, tm > 0, tm < times - 1, lax.rem(tm, 2) == 0


def framed(ref):
    return lambda s, i: ref[s, rows(i), :]


def apply_k(load, dst, planes, has_above, has_below, tiles=range(TILES)):
    row = row_iota()
    lane = lax.broadcasted_iota(jnp.int32, (8, 128), 1)
    for s, d in planes:
        cur = load(s, tiles[0])
        prev = load(s, tiles[0] - 1) if tiles[0] > 0 else cur
        for i in tiles:
            nxt = load(s, i + 1) if i < BOTTOM else cur
            up = up_roll(jnp.where(row == 7, prev, cur), 1)
            down = up_roll(jnp.where(row == 0, nxt, cur), 7)
            left = pltpu.roll(cur, 1, 1)
            right = pltpu.roll(cur, COLUMNS - 1, 1)
            left = jnp.concatenate([jnp.where(lane == 0, 0.0, left[:, :128]), left[:, 128:]], axis=1)
            right = jnp.concatenate(
                [right[:, :-128], jnp.where(lane == 127, 0.0, right[:, -128:])], axis=1
            )
            out = DIAG * cur - ((up + down) + (left + right))
            if i == 0:
                out = jnp.where(has_above, out, 0.0)
            if i == BOTTOM:
                out = jnp.where(has_below, out, 0.0)
            dst[d, rows(i), :] = out
            prev, cur = cur, nxt


def day_weights(has_before, has_after):
    first = jnp.where(has_before, INNER, prior_scale).astype(jnp.float32)
    last = jnp.where(has_after, INNER, prior_scale).astype(jnp.float32)
    return [first] + [jnp.float32(INNER)] * (DAYS - 2) + [last]


def intensity_kernel(
    offset, latent, counts, exposure, lat, exc, inten, head, tail, cnt, exposed, sems
):
    days = [
        (
            pltpu.make_async_copy(latent.at[t], lat.at[t], sems.at[3 * t]),
            pltpu.make_async_copy(exposure.at[t], exposed.at[t], sems.at[3 * t + 1]),
            pltpu.make_async_copy(counts.at[t], cnt.at[t], sems.at[3 * t + 2]),
        )
        for t in range(DAYS)
    ]
    for copies in days:
        for copy in copies:
            copy.start()
    row = row_iota()
    offsets = [
        jnp.concatenate([offset[rows(i), :]] * (COLUMNS // 128), axis=1) for i in range(OWN // 8)
    ]
    for t in range(DAYS):
        for copy in days[t]:
            copy.wait()
        for i in range(OWN // 8):
            value = exposed[t, rows(i), :] * jnp.exp(offsets[i] + lat[t, rows(i), :])
            inten[t, rows(i), :] = value
            exc[t, rows(i), :] = value - cnt[t, rows(i), :].astype(jnp.float32)
    last = OWN // 8 - 1
    for t in range(DAYS):
        tail[rows(t), :] = jnp.where(row < 2, up_roll(inten[t, rows(last), :], 2), lat[t, rows(last), :])
        head[rows(t), :] = jnp.where(row >= 6, up_roll(inten[t, rows(0), :], 6), lat[t, rows(0), :])
    for k in range(DAYS // 2):
        a, b = 2 * k, 2 * k + 1
        tail[rows(DAYS + k), :] = jnp.where(
            row >= 4, exc[a, rows(last), :], up_roll(exc[b, rows(last), :], 4)
        )
        head[rows(DAYS + k), :] = jnp.where(row < 4, exc[a, rows(0), :], up_roll(exc[b, rows(0), :], 4))


def residual_kernel(latent, inten, exc, above, below, lat, res, inner, y_msg, c_msg, tmp):
    has_above, has_below, has_before, has_after, even = places()
    row = row_iota()

    def field(t, i):
        if i in OWN_TILES:
            return latent[t, rows(i - 1), :]
        return (above if i == 0 else below)[rows(t), :]

    same = [(t, t) for t in range(DAYS)]
    apply_k(field, tmp, same, has_above, has_below)
    apply_k(framed(tmp), lat, same, has_above, has_below)
    weight = day_weights(has_before, has_after)

    for i in range(TILES):
        s = [lat[t, rows(i), :] for t in range(DAYS)]
        for t in range(DAYS):
            if i in (0, BOTTOM):
                excess = (above if i == 0 else below)[rows(DAYS + t // 2), :]
                excess = up_roll(excess, 4) if t % 2 else excess
            else:
                excess = exc[t, rows(i - 1), :]
            value = weight[t] * s[t] + excess
            if t > 0:
                value = value - COUPLE * s[t - 1]
            if t < DAYS - 1:
                value = value - COUPLE * s[t + 1]
            res[t, rows(i), :] = -value
    middle = range(DAYS - 2)
    apply_k(framed(res), tmp, [(k + 1, k) for k in middle], has_above, has_below)
    apply_k(framed(tmp), inner, [(k, k) for k in middle], has_above, has_below)

    def send(at, before, after):
        y_msg[rows(at), :] = jnp.where(even, before, after)
        c_msg[rows(at), :] = jnp.where(even, after, before)

    def halo(field, day):
        return jnp.where(row < 4, field[day, rows(BOTTOM), :], field[day, rows(0), :])

    first, last = 0, DAYS - 1
    for i in OWN_TILES:
        send(S_AT + i, lat[first, rows(i), :], lat[last, rows(i), :])
        send(R_AT + i, res[first, rows(i), :], res[last, rows(i), :])
        send(Q_AT + i - 1, -COUPLE * inner[0, rows(i), :], -COUPLE * inner[DAYS - 3, rows(i), :])
        send(I_AT + i - 1, inten[first, rows(i - 1), :], inten[last, rows(i - 1), :])
    send(S_AT, halo(lat, first), halo(lat, last))
    send(R_AT, halo(res, first), halo(res, last))
    outer = (row < 2) | (row >= 6)

    def slim(day, near):
        wanted = jnp.where(row < 4, up_roll(above[rows(day), :], 2), up_roll(below[rows(day), :], 6))
        return jnp.where(outer, -COUPLE * halo(inner, near), wanted)

    send(H_AT, slim(first, 0), slim(last, DAYS - 3))


def image_kernel(
    res, inner, lat, inten, above, below, y_msg, c_msg, u_out, q_out, z_out, sets, r6, q6, f6, tmp
):
    has_above, has_below, has_before, has_after, even = places()
    weight = day_weights(has_before, has_after)
    last = DAYS + 1

    def got(at):
        y, c = y_msg[rows(at), :], c_msg[rows(at), :]
        return jnp.where(even, y, c), jnp.where(even, c, y)

    for i in range(TILES):
        k = i if i in OWN_TILES else 0
        s_before, s_after = got(S_AT + k)
        r_before, r_after = got(R_AT + k)
        r6[0, rows(i), :] = jnp.where(has_before, r_before + COUPLE * lat[0, rows(i), :], 0.0)
        r6[last, rows(i), :] = jnp.where(has_after, r_after + COUPLE * lat[DAYS - 1, rows(i), :], 0.0)
        r6[1, rows(i), :] = res[0, rows(i), :] + COUPLE * s_before
        r6[DAYS, rows(i), :] = res[DAYS - 1, rows(i), :] + COUPLE * s_after
    outer = [(0, 0), (1, 1), (DAYS, DAYS), (last, last)]
    apply_k(framed(r6), tmp, outer, has_above, has_below)
    apply_k(framed(tmp), f6, outer, has_above, has_below)

    def residual(t, i):
        return r6[t, rows(i), :] if (t, t) in outer else res[t - 1, rows(i), :]

    def intensity(t, i):
        if i in OWN_TILES:
            return inten[t, rows(i - 1), :]
        return up_roll(above[rows(t), :], 6) if i == 0 else up_roll(below[rows(t), :], 2)

    for i in range(TILES):
        f = [
            f6[t, rows(i), :] if (t, t) in outer else inner[t - 2, rows(i), :]
            for t in range(DAYS + 2)
        ]
        r = [residual(t, i) for t in range(DAYS + 2)]
        for t in range(DAYS):
            q6[t + 1, rows(i), :] = (
                weight[t] * f[t + 1] - COUPLE * (f[t] + f[t + 2]) + intensity(t, i) * r[t + 1]
            )
        if i in OWN_TILES:
            q_side, i_side = got(Q_AT + i - 1), got(I_AT + i - 1)
        else:
            q_side = got(H_AT)
            i_side = [up_roll(v, 4) for v in q_side]
        before = INNER * f[0] - COUPLE * f[1] + q_side[0] + i_side[0] * r[0]
        after = INNER * f[last] - COUPLE * f[DAYS] + q_side[1] + i_side[1] * r[last]
        q6[0, rows(i), :] = jnp.where(has_before, before, 0.0)
        q6[last, rows(i), :] = jnp.where(has_after, after, 0.0)
    every = [(t, t) for t in range(DAYS + 2)]
    apply_k(framed(q6), tmp, every, has_above, has_below)
    apply_k(framed(tmp), f6, every, has_above, has_below, OWN_TILES)
    zero = jnp.zeros((8, COLUMNS), jnp.float32)

    uu = uq = zero
    for i in OWN_TILES:
        f = [f6[t, rows(i), :] for t in range(DAYS + 2)]
        for t in range(DAYS):
            q, u = q6[t + 1, rows(i), :], residual(t + 1, i)
            z = weight[t] * f[t + 1] - COUPLE * (f[t] + f[t + 2]) + intensity(t, i) * q
            z_out[t, rows(i - 1), :] = z
            q_out[t, rows(i - 1), :] = q
            u_out[t, rows(i - 1), :] = u
            uu = uu + u * u
            uq = uq + u * q

    def total(v):
        return jnp.sum(jnp.sum(v, axis=0, keepdims=True), axis=1, keepdims=True)

    uu, uq = total(uu), total(uq)
    ratio = jnp.where(uu > 0, uq / uu, 0.0)
    uw = ww = uy = wy = zero
    for i in range(OWN // 8):
        for t in range(DAYS):
            u, q, z = u_out[t, rows(i), :], q_out[t, rows(i), :], z_out[t, rows(i), :]
            w = q - ratio * u
            y = z - ratio * q
            uw, ww, uy, wy = uw + u * w, ww + w * w, uy + u * y, wy + w * y
    write_sets(sets, [uu, total(uw), total(ww), total(uy), total(wy), ratio])


def write_sets(sets, values):
    row = lax.broadcasted_iota(jnp.int32, (8, 128), 0)
    out = jnp.zeros((8, 128), jnp.float32)
    for k, value in enumerate(values):
        out = jnp.where(row == k, value, out)
    for n in range(sets.shape[0] // 8):
        sets[rows(n), :] = out


def recentred(got):
    senders = got.shape[0] // 8
    uu, uw, ww, uy, wy, ratio = (got[pl.ds(k, senders, 8), :] for k in range(6))

    def add(v):
        return jnp.sum(v, axis=0, keepdims=True)

    total = add(uu)
    centre = jnp.where(total > 0, add(uw + ratio * uu) / total, 0.0)
    e = ratio - centre
    uw_new = uw + e * uu
    ww_new = ww + e * (2.0 * uw + e * uu)
    uy_new = uy + e * uw + e * ratio * uu
    wy_new = wy + e * (ww + ratio * uw + uy) + e * e * (uw + ratio * uu)
    return total, add(uw_new), add(ww_new), add(uy_new), add(wy_new), centre


def regroup_kernel(got, sets):
    write_sets(sets, recentred(got))


def update_kernel(got, latent, u_in, q_in, z_in, updated, residual, new, left, sems):
    m0, _, ww, _, wy, centre = (v[:, :1] for v in recentred(got))
    alpha0 = 1.0 / centre
    norm1 = alpha0 * alpha0 * ww
    beta = norm1 / m0
    curvature1 = alpha0 * alpha0 * wy - beta * beta * (centre * m0)
    alpha1 = norm1 / curvature1
    copies = []
    for t in range(DAYS):
        for i in range(OWN // 8):
            u, q, z = u_in[t, rows(i), :], q_in[t, rows(i), :], z_in[t, rows(i), :]
            residual1 = u - alpha0 * q
            direction1 = residual1 + beta * u
            image1 = (q - alpha0 * z) + beta * q
            new[t, rows(i), :] = latent[t, rows(i), :] + (alpha0 * u + alpha1 * direction1)
            left[t, rows(i), :] = residual1 - alpha1 * image1
        copies += [
            pltpu.make_async_copy(new.at[t], updated.at[t], sems.at[2 * t]),
            pltpu.make_async_copy(left.at[t], residual.at[t], sems.at[2 * t + 1]),
        ]
        copies[-2].start()
        copies[-1].start()
    for copy in copies:
        copy.wait()


def gathered(sets, axis):
    count = lax.axis_size(axis)
    got = lax.all_to_all(sets.reshape(count, 8, 128), axis, 0, 0)
    return got.reshape(8 * count, 128)


def body(latent, counts, exposure, region_ids, coefficients):
    spaces, times = lax.axis_size("space"), lax.axis_size("tm")
    field, four = f32(DAYS, OWN, COLUMNS), f32(DAYS, FRAME, COLUMNS)
    edge, message = f32(EDGE, COLUMNS), f32(8 * MESSAGE_TILES, COLUMNS)

    def vmem(shape, dtype=jnp.float32):
        return pltpu.VMEM(shape, dtype)

    region = jnp.repeat(region_ids, REGION_ROWS)
    one_hot = region[:, None] == jnp.arange(coefficients.shape[0])[None, :]
    offset = jnp.sum(jnp.where(one_hot, coefficients[None, :], 0.0), axis=1)
    offset = jnp.broadcast_to(offset[:, None], (OWN, 128))

    lat, exc, inten, head, tail = pl.pallas_call(
        intensity_kernel,
        out_shape=(field, field, field, edge, edge),
        in_specs=[VMEM] + [HBM] * 3,
        out_specs=(VMEM,) * 5,
        scratch_shapes=[
            vmem(counts.shape, jnp.int32),
            vmem(exposure.shape),
            pltpu.SemaphoreType.DMA((3 * DAYS,)),
        ],
        compiler_params=FETCHING,
        name="intensity",
    )(offset, latent, counts, exposure)

    above = lax.ppermute(tail, "space", [(i, i + 1) for i in range(spaces - 1)])
    below = lax.ppermute(head, "space", [(i + 1, i) for i in range(spaces - 1)])

    spatial, res, inner, y_msg, c_msg = pl.pallas_call(
        residual_kernel,
        out_shape=(four, four, f32(DAYS - 2, FRAME, COLUMNS), message, message),
        in_specs=[VMEM] * 5,
        out_specs=(VMEM,) * 5,
        scratch_shapes=[vmem(four.shape)],
        compiler_params=PARAMS,
        name="residual",
    )(lat, inten, exc, above, below)

    across = [p for i in range(1, times - 1, 2) for p in ((i, i + 1), (i + 1, i))]
    within = [p for i in range(0, times - 1, 2) for p in ((i, i + 1), (i + 1, i))]
    y_got = lax.ppermute(y_msg, "tm", across)
    c_got = lax.ppermute(c_msg, "tm", within)

    six = vmem((DAYS + 2, FRAME, COLUMNS))
    u, q, z, sets = pl.pallas_call(
        image_kernel,
        out_shape=(field, field, field, f32(8 * times, 128)),
        in_specs=[VMEM] * 8,
        out_specs=(VMEM,) * 4,
        scratch_shapes=[six] * 4,
        compiler_params=PARAMS,
        name="image",
    )(res, inner, spatial, inten, above, below, y_got, c_got)

    sets = pl.pallas_call(
        regroup_kernel,
        out_shape=f32(8 * spaces, 128),
        in_specs=[VMEM],
        out_specs=VMEM,
        compiler_params=PARAMS,
        name="regroup",
    )(gathered(sets, "tm"))

    return pl.pallas_call(
        update_kernel,
        out_shape=(field, field),
        in_specs=[VMEM] * 5,
        out_specs=(HBM, HBM),
        scratch_shapes=[
            vmem(latent.shape),
            vmem(latent.shape),
            pltpu.SemaphoreType.DMA((2 * DAYS,)),
        ],
        compiler_params=PARAMS,
        name="update",
    )(gathered(sets, "space"), latent, u, q, z)


def solution(mesh):
    return jax.shard_map(
        body,
        mesh=mesh,
        in_specs=(
            P("tm", "space", None),
            P("tm", "space", None),
            P("tm", "space", None),
            P("space"),
            P(),
        ),
        out_specs=(P("tm", "space", None), P("tm", "space", None)),
        check_vma=False,
    )
```

```python
import functools

import jax
import jax.numpy as jnp
from jax import lax
from jax.experimental import pallas as pl
from jax.experimental.pallas import tpu as pltpu
from jax.sharding import PartitionSpec as P

kappa_square = 0.3
time_corr = 0.9
prior_scale = 0.05

COUPLE = prior_scale * time_corr
INNER = prior_scale * (1.0 + time_corr * time_corr)
DIAG = kappa_square + 4.0

DAYS, OWN, COLUMNS = 4, 32, 1024
TILES = OWN // 8 + 2
FRAME = 8 * TILES
BOTTOM = TILES - 1
OWN_TILES = range(1, BOTTOM)
REGION_ROWS = 4
EDGE = 8 * (DAYS + DAYS // 2)
MESSAGE_TILES = 2 * (OWN // 8 + 1) + 2 * (OWN // 8) + 1
S_AT, R_AT, Q_AT, I_AT, H_AT = 0, 5, 10, 14, 18

VMEM = pl.BlockSpec(memory_space=pltpu.VMEM)
HBM = pl.BlockSpec(memory_space=pltpu.HBM)
PARAMS = pltpu.CompilerParams(vmem_limit_bytes=40 * 1024 * 1024)
FETCHING = pltpu.CompilerParams(vmem_limit_bytes=53000 * 1024)


def f32(*shape):
    return jax.ShapeDtypeStruct(shape, jnp.float32)


def rows(i):
    return slice(8 * i, 8 * i + 8)


def row_iota():
    return lax.broadcasted_iota(jnp.int32, (8, COLUMNS), 0)


def up_roll(v, k):
    return pltpu.roll(v, k, 0)


def places():
    sp, tm = lax.axis_index("space"), lax.axis_index("tm")
    spaces, times = lax.axis_size("space"), lax.axis_size("tm")
    return sp > 0, sp < spaces - 1, tm > 0, tm < times - 1, lax.rem(tm, 2) == 0


def framed(ref):
    return lambda s, i: ref[s, rows(i), :]


class Either:
    def __init__(self, which, first, second):
        self.which, self.first, self.second = which, first, second

    def __getitem__(self, at):
        return jnp.where(self.which, self.first[at], self.second[at])


def alike():
    return lax.rem(lax.axis_index("space") + lax.axis_index("tm"), 2) == 0


def edges(first, second):
    return Either(alike(), second, first), Either(alike(), first, second)


def apply_k(load, dst, planes, has_above, has_below, tiles=range(TILES)):
    row = row_iota()
    lane = lax.broadcasted_iota(jnp.int32, (8, 128), 1)
    for s, d in planes:
        cur = load(s, tiles[0])
        prev = load(s, tiles[0] - 1) if tiles[0] > 0 else cur
        for i in tiles:
            nxt = load(s, i + 1) if i < BOTTOM else cur
            up = up_roll(jnp.where(row == 7, prev, cur), 1)
            down = up_roll(jnp.where(row == 0, nxt, cur), 7)
            left = pltpu.roll(cur, 1, 1)
            right = pltpu.roll(cur, COLUMNS - 1, 1)
            left = jnp.concatenate([jnp.where(lane == 0, 0.0, left[:, :128]), left[:, 128:]], axis=1)
            right = jnp.concatenate(
                [right[:, :-128], jnp.where(lane == 127, 0.0, right[:, -128:])], axis=1
            )
            out = DIAG * cur - ((up + down) + (left + right))
            if i == 0:
                out = jnp.where(has_above, out, 0.0)
            if i == BOTTOM:
                out = jnp.where(has_below, out, 0.0)
            dst[d, rows(i), :] = out
            prev, cur = cur, nxt


def day_weights(has_before, has_after):
    first = jnp.where(has_before, INNER, prior_scale).astype(jnp.float32)
    last = jnp.where(has_after, INNER, prior_scale).astype(jnp.float32)
    return [first] + [jnp.float32(INNER)] * (DAYS - 2) + [last]


def intensity_kernel(
    offset, latent, counts, exposure, lat, exc, inten, z_first, z_second, cnt, exposed, sems
):
    same = alike()

    def send(at, tail, head):
        z_first[rows(at), :] = jnp.where(same, tail, head)
        z_second[rows(at), :] = jnp.where(same, head, tail)

    days = [
        (
            pltpu.make_async_copy(latent.at[t], lat.at[t], sems.at[3 * t]),
            pltpu.make_async_copy(exposure.at[t], exposed.at[t], sems.at[3 * t + 1]),
            pltpu.make_async_copy(counts.at[t], cnt.at[t], sems.at[3 * t + 2]),
        )
        for t in range(DAYS)
    ]
    for copies in days:
        for copy in copies:
            copy.start()
    row = row_iota()
    blocks = 8 // REGION_ROWS
    offsets = []
    for i in range(OWN // 8):
        first, second = (offset[blocks * i + k : blocks * i + k + 1, :] for k in range(blocks))
        tile = jnp.where(row[:, :128] < REGION_ROWS, first, second)
        offsets.append(jnp.concatenate([tile] * (COLUMNS // 128), axis=1))
    for t in range(DAYS):
        for copy in days[t]:
            copy.wait()
        for i in range(OWN // 8):
            value = exposed[t, rows(i), :] * jnp.exp(offsets[i] + lat[t, rows(i), :])
            inten[t, rows(i), :] = value
            exc[t, rows(i), :] = value - cnt[t, rows(i), :].astype(jnp.float32)
    last = OWN // 8 - 1
    for t in range(DAYS):
        send(
            t,
            jnp.where(row < 2, up_roll(inten[t, rows(last), :], 2), lat[t, rows(last), :]),
            jnp.where(row >= 6, up_roll(inten[t, rows(0), :], 6), lat[t, rows(0), :]),
        )
    for k in range(DAYS // 2):
        a, b = 2 * k, 2 * k + 1
        send(
            DAYS + k,
            jnp.where(row >= 4, exc[a, rows(last), :], up_roll(exc[b, rows(last), :], 4)),
            jnp.where(row < 4, exc[a, rows(0), :], up_roll(exc[b, rows(0), :], 4)),
        )


def residual_kernel(latent, inten, exc, z_first, z_second, lat, res, inner, y_msg, c_msg, tmp):
    has_above, has_below, has_before, has_after, even = places()
    above, below = edges(z_first, z_second)
    row = row_iota()

    def field(t, i):
        if i in OWN_TILES:
            return latent[t, rows(i - 1), :]
        return (above if i == 0 else below)[rows(t), :]

    same = [(t, t) for t in range(DAYS)]
    apply_k(field, tmp, same, has_above, has_below)
    apply_k(framed(tmp), lat, same, has_above, has_below)
    weight = day_weights(has_before, has_after)

    for i in range(TILES):
        s = [lat[t, rows(i), :] for t in range(DAYS)]
        for t in range(DAYS):
            if i in (0, BOTTOM):
                excess = (above if i == 0 else below)[rows(DAYS + t // 2), :]
                excess = up_roll(excess, 4) if t % 2 else excess
            else:
                excess = exc[t, rows(i - 1), :]
            value = weight[t] * s[t] + excess
            if t > 0:
                value = value - COUPLE * s[t - 1]
            if t < DAYS - 1:
                value = value - COUPLE * s[t + 1]
            res[t, rows(i), :] = -value
    middle = range(DAYS - 2)
    apply_k(framed(res), tmp, [(k + 1, k) for k in middle], has_above, has_below)
    apply_k(framed(tmp), inner, [(k, k) for k in middle], has_above, has_below)

    def send(at, before, after):
        y_msg[rows(at), :] = jnp.where(even, before, after)
        c_msg[rows(at), :] = jnp.where(even, after, before)

    def halo(field, day):
        return jnp.where(row < 4, field[day, rows(BOTTOM), :], field[day, rows(0), :])

    first, last = 0, DAYS - 1
    for i in OWN_TILES:
        send(S_AT + i, lat[first, rows(i), :], lat[last, rows(i), :])
        send(R_AT + i, res[first, rows(i), :], res[last, rows(i), :])
        send(Q_AT + i - 1, -COUPLE * inner[0, rows(i), :], -COUPLE * inner[DAYS - 3, rows(i), :])
        send(I_AT + i - 1, inten[first, rows(i - 1), :], inten[last, rows(i - 1), :])
    send(S_AT, halo(lat, first), halo(lat, last))
    send(R_AT, halo(res, first), halo(res, last))
    outer = (row < 2) | (row >= 6)

    def slim(day, near):
        wanted = jnp.where(row < 4, up_roll(above[rows(day), :], 2), up_roll(below[rows(day), :], 6))
        return jnp.where(outer, -COUPLE * halo(inner, near), wanted)

    send(H_AT, slim(first, 0), slim(last, DAYS - 3))


def image_kernel(
    res, inner, lat, inten, z_first, z_second, y_msg, c_msg, u_out, q_out, z_out, sets, r6, mixed, f6, tmp
):
    has_above, has_below, has_before, has_after, even = places()
    above, below = edges(z_first, z_second)
    weight = day_weights(has_before, has_after)
    last = DAYS + 1

    def got(at):
        y, c = y_msg[rows(at), :], c_msg[rows(at), :]
        return jnp.where(even, y, c), jnp.where(even, c, y)

    for i in range(TILES):
        k = i if i in OWN_TILES else 0
        s_before, s_after = got(S_AT + k)
        r_before, r_after = got(R_AT + k)
        r6[0, rows(i), :] = jnp.where(has_before, r_before + COUPLE * lat[0, rows(i), :], 0.0)
        r6[last, rows(i), :] = jnp.where(has_after, r_after + COUPLE * lat[DAYS - 1, rows(i), :], 0.0)
        r6[1, rows(i), :] = res[0, rows(i), :] + COUPLE * s_before
        r6[DAYS, rows(i), :] = res[DAYS - 1, rows(i), :] + COUPLE * s_after
    outer = [(0, 0), (1, 1), (DAYS, DAYS), (last, last)]
    apply_k(framed(r6), tmp, outer, has_above, has_below)
    apply_k(framed(tmp), f6, outer, has_above, has_below)

    def residual(t, i):
        return r6[t, rows(i), :] if (t, t) in outer else res[t - 1, rows(i), :]

    def intensity(t, i):
        if i in OWN_TILES:
            return inten[t, rows(i - 1), :]
        return up_roll(above[rows(t), :], 6) if i == 0 else up_roll(below[rows(t), :], 2)

    for i in range(TILES):
        f = [
            f6[t, rows(i), :] if (t, t) in outer else inner[t - 2, rows(i), :]
            for t in range(DAYS + 2)
        ]
        r = [residual(t, i) for t in range(DAYS + 2)]
        if i in OWN_TILES:
            q_side, i_side = got(Q_AT + i - 1), got(I_AT + i - 1)
        else:
            q_side = got(H_AT)
            i_side = [up_roll(v, 4) for v in q_side]
        before = INNER * f[0] - COUPLE * f[1] + q_side[0] + i_side[0] * r[0]
        after = INNER * f[last] - COUPLE * f[DAYS] + q_side[1] + i_side[1] * r[last]
        q = [jnp.where(has_before, before, 0.0)]
        for t in range(DAYS):
            q.append(weight[t] * f[t + 1] - COUPLE * (f[t] + f[t + 2]) + intensity(t, i) * r[t + 1])
        q.append(jnp.where(has_after, after, 0.0))
        for t in range(DAYS):
            mixed[t, rows(i), :] = weight[t] * q[t + 1] - COUPLE * (q[t] + q[t + 2])
            if i in OWN_TILES:
                q_out[t, rows(i - 1), :] = q[t + 1]
    days = [(t, t) for t in range(DAYS)]
    apply_k(framed(mixed), tmp, days, has_above, has_below)
    apply_k(framed(tmp), mixed, days, has_above, has_below, OWN_TILES)
    zero = jnp.zeros((8, COLUMNS), jnp.float32)

    uu = uq = zero
    for i in OWN_TILES:
        for t in range(DAYS):
            q, u = q_out[t, rows(i - 1), :], residual(t + 1, i)
            z_out[t, rows(i - 1), :] = mixed[t, rows(i), :] + intensity(t, i) * q
            u_out[t, rows(i - 1), :] = u
            uu = uu + u * u
            uq = uq + u * q

    def total(v):
        return jnp.sum(jnp.sum(v, axis=0, keepdims=True), axis=1, keepdims=True)

    uu, uq = total(uu), total(uq)
    ratio = jnp.where(uu > 0, uq / uu, 0.0)
    uw = ww = uy = wy = zero
    for i in range(OWN // 8):
        for t in range(DAYS):
            u, q, z = u_out[t, rows(i), :], q_out[t, rows(i), :], z_out[t, rows(i), :]
            w = q - ratio * u
            y = z - ratio * q
            uw, ww, uy, wy = uw + u * w, ww + w * w, uy + u * y, wy + w * y
    write_sets(sets, [uu, total(uw), total(ww), total(uy), total(wy), ratio])


def write_sets(sets, values):
    row = lax.broadcasted_iota(jnp.int32, (8, 128), 0)
    out = jnp.zeros((8, 128), jnp.float32)
    for k, value in enumerate(values):
        out = jnp.where(row == k, value, out)
    for n in range(sets.shape[0] // 8):
        sets[rows(n), :] = out


def recentred(got):
    senders = got.shape[0] // 8
    uu, uw, ww, uy, wy, ratio = (got[pl.ds(k, senders, 8), :] for k in range(6))

    def add(v):
        return jnp.sum(v, axis=0, keepdims=True)

    total = add(uu)
    centre = jnp.where(total > 0, add(uw + ratio * uu) / total, 0.0)
    e = ratio - centre
    uw_new = uw + e * uu
    ww_new = ww + e * (2.0 * uw + e * uu)
    uy_new = uy + e * uw + e * ratio * uu
    wy_new = wy + e * (ww + ratio * uw + uy) + e * e * (uw + ratio * uu)
    return total, add(uw_new), add(ww_new), add(uy_new), add(wy_new), centre


def regroup_kernel(got, sets):
    write_sets(sets, recentred(got))


def update_kernel(got, latent, u_in, q_in, z_in, updated, residual, new, left, sems):
    m0, _, ww, _, wy, centre = (v[:, :1] for v in recentred(got))
    alpha0 = 1.0 / centre
    norm1 = alpha0 * alpha0 * ww
    beta = norm1 / m0
    curvature1 = alpha0 * alpha0 * wy - beta * beta * (centre * m0)
    alpha1 = norm1 / curvature1
    copies = []
    for t in range(DAYS):
        for i in range(OWN // 8):
            u, q, z = u_in[t, rows(i), :], q_in[t, rows(i), :], z_in[t, rows(i), :]
            residual1 = u - alpha0 * q
            direction1 = residual1 + beta * u
            image1 = (q - alpha0 * z) + beta * q
            new[t, rows(i), :] = latent[t, rows(i), :] + (alpha0 * u + alpha1 * direction1)
            left[t, rows(i), :] = residual1 - alpha1 * image1
        copies += [
            pltpu.make_async_copy(new.at[t], updated.at[t], sems.at[2 * t]),
            pltpu.make_async_copy(left.at[t], residual.at[t], sems.at[2 * t + 1]),
        ]
        copies[-2].start()
        copies[-1].start()
    for copy in copies:
        copy.wait()


def gathered(sets, axis):
    count = lax.axis_size(axis)
    got = lax.all_to_all(sets.reshape(count, 8, 128), axis, 0, 0)
    return got.reshape(8 * count, 128)


def body(latent, counts, exposure, region_ids, coefficients):
    spaces, times = lax.axis_size("space"), lax.axis_size("tm")
    field, four = f32(DAYS, OWN, COLUMNS), f32(DAYS, FRAME, COLUMNS)
    edge, message = f32(EDGE, COLUMNS), f32(8 * MESSAGE_TILES, COLUMNS)

    def vmem(shape, dtype=jnp.float32):
        return pltpu.VMEM(shape, dtype)

    one_hot = region_ids[:, None, None] == jnp.arange(coefficients.shape[0])[None, :, None]
    offset = jnp.where(one_hot, coefficients[None, :, None], 0.0)
    offset = jnp.sum(jnp.broadcast_to(offset, offset.shape[:2] + (128,)), axis=1)

    lat, exc, inten, z_first, z_second = pl.pallas_call(
        intensity_kernel,
        out_shape=(field, field, field, edge, edge),
        in_specs=[VMEM] + [HBM] * 3,
        out_specs=(VMEM,) * 5,
        scratch_shapes=[
            vmem(counts.shape, jnp.int32),
            vmem(exposure.shape),
            pltpu.SemaphoreType.DMA((3 * DAYS,)),
        ],
        compiler_params=FETCHING,
        name="intensity",
    )(offset, latent, counts, exposure)

    def pairs(count, first):
        return [p for i in range(first, count - 1, 2) for p in ((i, i + 1), (i + 1, i))]

    def turns(k):
        return [
            (t * spaces + i, t * spaces + j)
            for t in range(times)
            for i, j in pairs(spaces, (t + k) % 2)
        ]

    z_first = lax.ppermute(z_first, ("tm", "space"), turns(0))
    z_second = lax.ppermute(z_second, ("tm", "space"), turns(1))

    spatial, res, inner, y_msg, c_msg = pl.pallas_call(
        residual_kernel,
        out_shape=(four, four, f32(DAYS - 2, FRAME, COLUMNS), message, message),
        in_specs=[VMEM] * 5,
        out_specs=(VMEM,) * 5,
        scratch_shapes=[vmem(four.shape)],
        compiler_params=PARAMS,
        name="residual",
    )(lat, inten, exc, z_first, z_second)

    y_got = lax.ppermute(y_msg, "tm", pairs(times, 1))
    c_got = lax.ppermute(c_msg, "tm", pairs(times, 0))

    six = vmem((DAYS + 2, FRAME, COLUMNS))
    u, q, z, sets = pl.pallas_call(
        image_kernel,
        out_shape=(field, field, field, f32(8 * times, 128)),
        in_specs=[VMEM] * 8,
        out_specs=(VMEM,) * 4,
        scratch_shapes=[six] * 4,
        compiler_params=PARAMS,
        name="image",
    )(res, inner, spatial, inten, z_first, z_second, y_got, c_got)

    sets = pl.pallas_call(
        regroup_kernel,
        out_shape=f32(8 * spaces, 128),
        in_specs=[VMEM],
        out_specs=VMEM,
        compiler_params=PARAMS,
        name="regroup",
    )(gathered(sets, "tm"))

    return pl.pallas_call(
        update_kernel,
        out_shape=(field, field),
        in_specs=[VMEM] * 5,
        out_specs=(HBM, HBM),
        scratch_shapes=[
            vmem(latent.shape),
            vmem(latent.shape),
            pltpu.SemaphoreType.DMA((2 * DAYS,)),
        ],
        compiler_params=PARAMS,
        name="update",
    )(gathered(sets, "space"), latent, u, q, z)


def solution(mesh):
    return jax.shard_map(
        body,
        mesh=mesh,
        in_specs=(
            P("tm", "space", None),
            P("tm", "space", None),
            P("tm", "space", None),
            P("space"),
            P(),
        ),
        out_specs=(P("tm", "space", None), P("tm", "space", None)),
        check_vma=False,
    )
```

```python
import functools

import jax
import jax.numpy as jnp
from jax import lax
from jax.experimental import pallas as pl
from jax.experimental.pallas import tpu as pltpu
from jax.sharding import PartitionSpec as P

kappa_square = 0.3
time_corr = 0.9
prior_scale = 0.05

COUPLE = prior_scale * time_corr
INNER = prior_scale * (1.0 + time_corr * time_corr)
DIAG = kappa_square + 4.0

DAYS, OWN, COLUMNS = 4, 32, 1024
TILES = OWN // 8 + 2
FRAME = 8 * TILES
BOTTOM = TILES - 1
OWN_TILES = range(1, BOTTOM)
REGION_ROWS = 4
EDGE = 8 * (DAYS + DAYS // 2)
MESSAGE_TILES = 2 * (OWN // 8 + 1) + 2 * (OWN // 8) + 1
S_AT, R_AT, Q_AT, I_AT, H_AT = 0, 5, 10, 14, 18

VMEM = pl.BlockSpec(memory_space=pltpu.VMEM)
HBM = pl.BlockSpec(memory_space=pltpu.HBM)
PARAMS = pltpu.CompilerParams(vmem_limit_bytes=40 * 1024 * 1024)
FETCHING = pltpu.CompilerParams(vmem_limit_bytes=53000 * 1024)


def f32(*shape):
    return jax.ShapeDtypeStruct(shape, jnp.float32)


def rows(i):
    return slice(8 * i, 8 * i + 8)


def row_iota():
    return lax.broadcasted_iota(jnp.int32, (8, COLUMNS), 0)


def up_roll(v, k):
    return pltpu.roll(v, k, 0)


def places():
    sp, tm = lax.axis_index("space"), lax.axis_index("tm")
    spaces, times = lax.axis_size("space"), lax.axis_size("tm")
    return sp > 0, sp < spaces - 1, tm > 0, tm < times - 1, lax.rem(tm, 2) == 0


def framed(ref):
    return lambda s, i: ref[s, rows(i), :]


class Either:
    def __init__(self, which, first, second):
        self.which, self.first, self.second = which, first, second

    def __getitem__(self, at):
        return jnp.where(self.which, self.first[at], self.second[at])


def alike():
    return lax.rem(lax.axis_index("space") + lax.axis_index("tm"), 2) == 0


def edges(first, second):
    return Either(alike(), second, first), Either(alike(), first, second)


def apply_k(load, dst, planes, has_above, has_below, tiles=range(TILES)):
    row = row_iota()
    lane = lax.broadcasted_iota(jnp.int32, (8, 128), 1)
    for s, d in planes:
        cur = load(s, tiles[0])
        prev = load(s, tiles[0] - 1) if tiles[0] > 0 else cur
        for i in tiles:
            nxt = load(s, i + 1) if i < BOTTOM else cur
            up = up_roll(jnp.where(row == 7, prev, cur), 1)
            down = up_roll(jnp.where(row == 0, nxt, cur), 7)
            left = pltpu.roll(cur, 1, 1)
            right = pltpu.roll(cur, COLUMNS - 1, 1)
            left = jnp.concatenate([jnp.where(lane == 0, 0.0, left[:, :128]), left[:, 128:]], axis=1)
            right = jnp.concatenate(
                [right[:, :-128], jnp.where(lane == 127, 0.0, right[:, -128:])], axis=1
            )
            out = DIAG * cur - ((up + down) + (left + right))
            if i == 0:
                out = jnp.where(has_above, out, 0.0)
            if i == BOTTOM:
                out = jnp.where(has_below, out, 0.0)
            dst[d, rows(i), :] = out
            prev, cur = cur, nxt


def day_weights(has_before, has_after):
    first = jnp.where(has_before, INNER, prior_scale).astype(jnp.float32)
    last = jnp.where(has_after, INNER, prior_scale).astype(jnp.float32)
    return [first] + [jnp.float32(INNER)] * (DAYS - 2) + [last]


def intensity_kernel(
    offset, latent, counts, exposure, lat, exc, inten, z_first, z_second, cnt, exposed, sems
):
    same = alike()

    def send(at, tail, head):
        z_first[rows(at), :] = jnp.where(same, tail, head)
        z_second[rows(at), :] = jnp.where(same, head, tail)

    days = [
        (
            pltpu.make_async_copy(latent.at[t], lat.at[t], sems.at[3 * t]),
            pltpu.make_async_copy(exposure.at[t], exposed.at[t], sems.at[3 * t + 1]),
            pltpu.make_async_copy(counts.at[t], cnt.at[t], sems.at[3 * t + 2]),
        )
        for t in range(DAYS)
    ]
    for copies in days:
        for copy in copies:
            copy.start()
    row = row_iota()
    blocks = 8 // REGION_ROWS
    offsets = []
    for i in range(OWN // 8):
        first, second = (offset[blocks * i + k : blocks * i + k + 1, :] for k in range(blocks))
        tile = jnp.where(row[:, :128] < REGION_ROWS, first, second)
        offsets.append(jnp.concatenate([tile] * (COLUMNS // 128), axis=1))
    for t in range(DAYS):
        for copy in days[t]:
            copy.wait()
        for i in range(OWN // 8):
            value = exposed[t, rows(i), :] * jnp.exp(offsets[i] + lat[t, rows(i), :])
            inten[t, rows(i), :] = value
            exc[t, rows(i), :] = value - cnt[t, rows(i), :].astype(jnp.float32)
    last = OWN // 8 - 1
    for t in range(DAYS):
        send(
            t,
            jnp.where(row < 2, up_roll(inten[t, rows(last), :], 2), lat[t, rows(last), :]),
            jnp.where(row >= 6, up_roll(inten[t, rows(0), :], 6), lat[t, rows(0), :]),
        )
    for k in range(DAYS // 2):
        a, b = 2 * k, 2 * k + 1
        send(
            DAYS + k,
            jnp.where(row >= 4, exc[a, rows(last), :], up_roll(exc[b, rows(last), :], 4)),
            jnp.where(row < 4, exc[a, rows(0), :], up_roll(exc[b, rows(0), :], 4)),
        )


def residual_kernel(latent, inten, exc, z_first, z_second, lat, res, inner, y_msg, c_msg, tmp):
    has_above, has_below, has_before, has_after, even = places()
    above, below = edges(z_first, z_second)
    row = row_iota()

    def field(t, i):
        if i in OWN_TILES:
            return latent[t, rows(i - 1), :]
        return (above if i == 0 else below)[rows(t), :]

    same = [(t, t) for t in range(DAYS)]
    apply_k(field, tmp, same, has_above, has_below)
    apply_k(framed(tmp), lat, same, has_above, has_below)
    weight = day_weights(has_before, has_after)

    for i in range(TILES):
        s = [lat[t, rows(i), :] for t in range(DAYS)]
        for t in range(DAYS):
            if i in (0, BOTTOM):
                excess = (above if i == 0 else below)[rows(DAYS + t // 2), :]
                excess = up_roll(excess, 4) if t % 2 else excess
            else:
                excess = exc[t, rows(i - 1), :]
            value = weight[t] * s[t] + excess
            if t > 0:
                value = value - COUPLE * s[t - 1]
            if t < DAYS - 1:
                value = value - COUPLE * s[t + 1]
            res[t, rows(i), :] = -value
    middle = range(DAYS - 2)
    apply_k(framed(res), tmp, [(k + 1, k) for k in middle], has_above, has_below)
    apply_k(framed(tmp), inner, [(k, k) for k in middle], has_above, has_below)

    def send(at, before, after):
        y_msg[rows(at), :] = jnp.where(even, before, after)
        c_msg[rows(at), :] = jnp.where(even, after, before)

    def halo(field, day):
        return jnp.where(row < 4, field[day, rows(BOTTOM), :], field[day, rows(0), :])

    first, last = 0, DAYS - 1
    for i in OWN_TILES:
        send(S_AT + i, lat[first, rows(i), :], lat[last, rows(i), :])
        send(R_AT + i, res[first, rows(i), :], res[last, rows(i), :])
        send(Q_AT + i - 1, -COUPLE * inner[0, rows(i), :], -COUPLE * inner[DAYS - 3, rows(i), :])
        send(I_AT + i - 1, inten[first, rows(i - 1), :], inten[last, rows(i - 1), :])
    send(S_AT, halo(lat, first), halo(lat, last))
    send(R_AT, halo(res, first), halo(res, last))
    outer = (row < 2) | (row >= 6)

    def slim(day, near):
        wanted = jnp.where(row < 4, up_roll(above[rows(day), :], 2), up_roll(below[rows(day), :], 6))
        return jnp.where(outer, -COUPLE * halo(inner, near), wanted)

    send(H_AT, slim(first, 0), slim(last, DAYS - 3))


def image_kernel(
    res, inner, lat, inten, z_first, z_second, y_msg, c_msg, u_out, q_out, z_out, sets, r6, mixed, f6, tmp
):
    has_above, has_below, has_before, has_after, even = places()
    above, below = edges(z_first, z_second)
    weight = day_weights(has_before, has_after)
    last = DAYS + 1

    def got(at):
        y, c = y_msg[rows(at), :], c_msg[rows(at), :]
        return jnp.where(even, y, c), jnp.where(even, c, y)

    for i in range(TILES):
        k = i if i in OWN_TILES else 0
        s_before, s_after = got(S_AT + k)
        r_before, r_after = got(R_AT + k)
        r6[0, rows(i), :] = jnp.where(has_before, r_before + COUPLE * lat[0, rows(i), :], 0.0)
        r6[last, rows(i), :] = jnp.where(has_after, r_after + COUPLE * lat[DAYS - 1, rows(i), :], 0.0)
        r6[1, rows(i), :] = res[0, rows(i), :] + COUPLE * s_before
        r6[DAYS, rows(i), :] = res[DAYS - 1, rows(i), :] + COUPLE * s_after
    outer = [(0, 0), (1, 1), (DAYS, DAYS), (last, last)]
    apply_k(framed(r6), tmp, outer, has_above, has_below)
    apply_k(framed(tmp), f6, outer, has_above, has_below)

    def residual(t, i):
        return r6[t, rows(i), :] if (t, t) in outer else res[t - 1, rows(i), :]

    def intensity(t, i):
        if i in OWN_TILES:
            return inten[t, rows(i - 1), :]
        return up_roll(above[rows(t), :], 6) if i == 0 else up_roll(below[rows(t), :], 2)

    for i in range(TILES):
        f = [
            f6[t, rows(i), :] if (t, t) in outer else inner[t - 2, rows(i), :]
            for t in range(DAYS + 2)
        ]
        r = [residual(t, i) for t in range(DAYS + 2)]
        if i in OWN_TILES:
            q_side, i_side = got(Q_AT + i - 1), got(I_AT + i - 1)
        else:
            q_side = got(H_AT)
            i_side = [up_roll(v, 4) for v in q_side]
        before = INNER * f[0] - COUPLE * f[1] + q_side[0] + i_side[0] * r[0]
        after = INNER * f[last] - COUPLE * f[DAYS] + q_side[1] + i_side[1] * r[last]
        q = [jnp.where(has_before, before, 0.0)]
        for t in range(DAYS):
            q.append(weight[t] * f[t + 1] - COUPLE * (f[t] + f[t + 2]) + intensity(t, i) * r[t + 1])
        q.append(jnp.where(has_after, after, 0.0))
        for t in range(DAYS):
            mixed[t, rows(i), :] = weight[t] * q[t + 1] - COUPLE * (q[t] + q[t + 2])
            if i in OWN_TILES:
                q_out[t, rows(i - 1), :] = q[t + 1]
    days = [(t, t) for t in range(DAYS)]
    apply_k(framed(mixed), tmp, days, has_above, has_below)
    apply_k(framed(tmp), mixed, days, has_above, has_below, OWN_TILES)
    zero = jnp.zeros((8, COLUMNS), jnp.float32)

    uu = uq = zero
    for i in OWN_TILES:
        for t in range(DAYS):
            q, u = q_out[t, rows(i - 1), :], residual(t + 1, i)
            z_out[t, rows(i - 1), :] = mixed[t, rows(i), :] + intensity(t, i) * q
            u_out[t, rows(i - 1), :] = u
            uu = uu + u * u
            uq = uq + u * q

    def total(v):
        return jnp.sum(jnp.sum(v, axis=0, keepdims=True), axis=1, keepdims=True)

    uu, uq = total(uu), total(uq)
    ratio = jnp.where(uu > 0, uq / uu, 0.0)
    uw = ww = uy = wy = zero
    for i in range(OWN // 8):
        for t in range(DAYS):
            u, q, z = u_out[t, rows(i), :], q_out[t, rows(i), :], z_out[t, rows(i), :]
            w = q - ratio * u
            y = z - ratio * q
            uw, ww, uy, wy = uw + u * w, ww + w * w, uy + u * y, wy + w * y
    write_sets(sets, [uu, total(uw), total(ww), total(uy), total(wy), ratio])


def write_sets(sets, values):
    lane = lax.broadcasted_iota(jnp.int32, (1, 128), 1)
    out = jnp.zeros((1, 128), jnp.float32)
    for k, value in enumerate(values):
        out = jnp.where(lane == k, value, out)
    sets[...] = jnp.broadcast_to(out, sets.shape)


def recentred(got):
    by_lane = got[...].T
    uu, uw, ww, uy, wy, ratio = (by_lane[k : k + 1, :] for k in range(6))

    def add(v):
        return jnp.sum(v, axis=1, keepdims=True)

    total = add(uu)
    centre = jnp.where(total > 0, add(uw + ratio * uu) / total, 0.0)
    e = ratio - centre
    uw_new = uw + e * uu
    ww_new = ww + e * (2.0 * uw + e * uu)
    uy_new = uy + e * uw + e * ratio * uu
    wy_new = wy + e * (ww + ratio * uw + uy) + e * e * (uw + ratio * uu)
    return total, add(uw_new), add(ww_new), add(uy_new), add(wy_new), centre


def regroup_kernel(got, sets):
    write_sets(sets, recentred(got))


def update_kernel(got, latent, u_in, q_in, z_in, updated, residual, new, left, sems):
    m0, _, ww, _, wy, centre = recentred(got)
    alpha0 = 1.0 / centre
    norm1 = alpha0 * alpha0 * ww
    beta = norm1 / m0
    curvature1 = alpha0 * alpha0 * wy - beta * beta * (centre * m0)
    alpha1 = norm1 / curvature1
    copies = []
    for t in range(DAYS):
        for i in range(OWN // 8):
            u, q, z = u_in[t, rows(i), :], q_in[t, rows(i), :], z_in[t, rows(i), :]
            residual1 = u - alpha0 * q
            direction1 = residual1 + beta * u
            image1 = (q - alpha0 * z) + beta * q
            new[t, rows(i), :] = latent[t, rows(i), :] + (alpha0 * u + alpha1 * direction1)
            left[t, rows(i), :] = residual1 - alpha1 * image1
        copies += [
            pltpu.make_async_copy(new.at[t], updated.at[t], sems.at[2 * t]),
            pltpu.make_async_copy(left.at[t], residual.at[t], sems.at[2 * t + 1]),
        ]
        copies[-2].start()
        copies[-1].start()
    for copy in copies:
        copy.wait()


def gathered(sets, axis):
    return lax.all_to_all(sets, axis, 0, 0)


def body(latent, counts, exposure, region_ids, coefficients):
    spaces, times = lax.axis_size("space"), lax.axis_size("tm")
    field, four = f32(DAYS, OWN, COLUMNS), f32(DAYS, FRAME, COLUMNS)
    edge, message = f32(EDGE, COLUMNS), f32(8 * MESSAGE_TILES, COLUMNS)

    def vmem(shape, dtype=jnp.float32):
        return pltpu.VMEM(shape, dtype)

    one_hot = region_ids[:, None, None] == jnp.arange(coefficients.shape[0])[None, :, None]
    offset = jnp.where(one_hot, coefficients[None, :, None], 0.0)
    offset = jnp.sum(jnp.broadcast_to(offset, offset.shape[:2] + (128,)), axis=1)

    lat, exc, inten, z_first, z_second = pl.pallas_call(
        intensity_kernel,
        out_shape=(field, field, field, edge, edge),
        in_specs=[VMEM] + [HBM] * 3,
        out_specs=(VMEM,) * 5,
        scratch_shapes=[
            vmem(counts.shape, jnp.int32),
            vmem(exposure.shape),
            pltpu.SemaphoreType.DMA((3 * DAYS,)),
        ],
        compiler_params=FETCHING,
        name="intensity",
    )(offset, latent, counts, exposure)

    def pairs(count, first):
        return [p for i in range(first, count - 1, 2) for p in ((i, i + 1), (i + 1, i))]

    def turns(k):
        return [
            (t * spaces + i, t * spaces + j)
            for t in range(times)
            for i, j in pairs(spaces, (t + k) % 2)
        ]

    z_first = lax.ppermute(z_first, ("tm", "space"), turns(0))
    z_second = lax.ppermute(z_second, ("tm", "space"), turns(1))

    spatial, res, inner, y_msg, c_msg = pl.pallas_call(
        residual_kernel,
        out_shape=(four, four, f32(DAYS - 2, FRAME, COLUMNS), message, message),
        in_specs=[VMEM] * 5,
        out_specs=(VMEM,) * 5,
        scratch_shapes=[vmem(four.shape)],
        compiler_params=PARAMS,
        name="residual",
    )(lat, inten, exc, z_first, z_second)

    y_got = lax.ppermute(y_msg, "tm", pairs(times, 1))
    c_got = lax.ppermute(c_msg, "tm", pairs(times, 0))

    six = vmem((DAYS + 2, FRAME, COLUMNS))
    u, q, z, sets = pl.pallas_call(
        image_kernel,
        out_shape=(field, field, field, f32(times, 128)),
        in_specs=[VMEM] * 8,
        out_specs=(VMEM,) * 4,
        scratch_shapes=[six] * 4,
        compiler_params=PARAMS,
        name="image",
    )(res, inner, spatial, inten, z_first, z_second, y_got, c_got)

    sets = pl.pallas_call(
        regroup_kernel,
        out_shape=f32(spaces, 128),
        in_specs=[VMEM],
        out_specs=VMEM,
        compiler_params=PARAMS,
        name="regroup",
    )(gathered(sets, "tm"))

    return pl.pallas_call(
        update_kernel,
        out_shape=(field, field),
        in_specs=[VMEM] * 5,
        out_specs=(HBM, HBM),
        scratch_shapes=[
            vmem(latent.shape),
            vmem(latent.shape),
            pltpu.SemaphoreType.DMA((2 * DAYS,)),
        ],
        compiler_params=PARAMS,
        name="update",
    )(gathered(sets, "space"), latent, u, q, z)


def solution(mesh):
    return jax.shard_map(
        body,
        mesh=mesh,
        in_specs=(
            P("tm", "space", None),
            P("tm", "space", None),
            P("tm", "space", None),
            P("space"),
            P(),
        ),
        out_specs=(P("tm", "space", None), P("tm", "space", None)),
        check_vma=False,
    )
```

```python
import functools

import jax
import jax.numpy as jnp
from jax import lax
from jax.experimental import pallas as pl
from jax.experimental.pallas import tpu as pltpu
from jax.sharding import PartitionSpec as P

kappa_square = 0.3
time_corr = 0.9
prior_scale = 0.05

COUPLE = prior_scale * time_corr
INNER = prior_scale * (1.0 + time_corr * time_corr)
DIAG = kappa_square + 4.0

DAYS, OWN, COLUMNS = 4, 32, 1024
TILES = OWN // 8 + 2
FRAME = 8 * TILES
BOTTOM = TILES - 1
OWN_TILES = range(1, BOTTOM)
REGION_ROWS = 4
EDGE = 8 * (DAYS + DAYS // 2)
MESSAGE_TILES = 2 * (OWN // 8 + 1) + 2 * (OWN // 8) + 1
S_AT, R_AT, Q_AT, I_AT, H_AT = 0, 5, 10, 14, 18

VMEM = pl.BlockSpec(memory_space=pltpu.VMEM)
HBM = pl.BlockSpec(memory_space=pltpu.HBM)
PARAMS = pltpu.CompilerParams(vmem_limit_bytes=40 * 1024 * 1024)
FETCHING = pltpu.CompilerParams(vmem_limit_bytes=53000 * 1024)


def f32(*shape):
    return jax.ShapeDtypeStruct(shape, jnp.float32)


def rows(i):
    return slice(8 * i, 8 * i + 8)


def row_iota():
    return lax.broadcasted_iota(jnp.int32, (8, COLUMNS), 0)


def up_roll(v, k):
    return pltpu.roll(v, k, 0)


def places():
    sp, tm = lax.axis_index("space"), lax.axis_index("tm")
    spaces, times = lax.axis_size("space"), lax.axis_size("tm")
    return sp > 0, sp < spaces - 1, tm > 0, tm < times - 1, lax.rem(tm, 2) == 0


def framed(ref):
    return lambda s, i: ref[s, rows(i), :]


class Either:
    def __init__(self, which, first, second):
        self.which, self.first, self.second = which, first, second

    def __getitem__(self, at):
        return jnp.where(self.which, self.first[at], self.second[at])


def unlike():
    return lax.rem(lax.axis_index("space") + lax.axis_index("tm"), 2) == 1


def edges(first, second):
    return Either(unlike(), second, first), Either(unlike(), first, second)


def apply_k(load, dst, planes, has_above, has_below, tiles=range(TILES)):
    row = row_iota()
    lane = lax.broadcasted_iota(jnp.int32, (8, 128), 1)
    for s, d in planes:
        cur = load(s, tiles[0])
        prev = load(s, tiles[0] - 1) if tiles[0] > 0 else cur
        for i in tiles:
            nxt = load(s, i + 1) if i < BOTTOM else cur
            up = up_roll(jnp.where(row == 7, prev, cur), 1)
            down = up_roll(jnp.where(row == 0, nxt, cur), 7)
            left = pltpu.roll(cur, 1, 1)
            right = pltpu.roll(cur, COLUMNS - 1, 1)
            left = jnp.concatenate([jnp.where(lane == 0, 0.0, left[:, :128]), left[:, 128:]], axis=1)
            right = jnp.concatenate(
                [right[:, :-128], jnp.where(lane == 127, 0.0, right[:, -128:])], axis=1
            )
            out = DIAG * cur - ((up + down) + (left + right))
            if i == 0:
                out = jnp.where(has_above, out, 0.0)
            if i == BOTTOM:
                out = jnp.where(has_below, out, 0.0)
            dst[d, rows(i), :] = out
            prev, cur = cur, nxt


def day_weights(has_before, has_after):
    first = jnp.where(has_before, INNER, prior_scale).astype(jnp.float32)
    last = jnp.where(has_after, INNER, prior_scale).astype(jnp.float32)
    return [first] + [jnp.float32(INNER)] * (DAYS - 2) + [last]


def intensity_kernel(
    offset, latent, counts, exposure, lat, exc, inten, z_first, z_second, cnt, exposed, sems
):
    same = unlike()

    def send(at, tail, head):
        z_first[rows(at), :] = jnp.where(same, tail, head)
        z_second[rows(at), :] = jnp.where(same, head, tail)

    days = [
        (
            pltpu.make_async_copy(latent.at[t], lat.at[t], sems.at[3 * t]),
            pltpu.make_async_copy(exposure.at[t], exposed.at[t], sems.at[3 * t + 1]),
            pltpu.make_async_copy(counts.at[t], cnt.at[t], sems.at[3 * t + 2]),
        )
        for t in range(DAYS)
    ]
    for copies in days:
        for copy in copies:
            copy.start()
    row = row_iota()
    blocks = 8 // REGION_ROWS
    offsets = []
    for i in range(OWN // 8):
        first, second = (offset[blocks * i + k : blocks * i + k + 1, :] for k in range(blocks))
        tile = jnp.where(row[:, :128] < REGION_ROWS, first, second)
        offsets.append(jnp.concatenate([tile] * (COLUMNS // 128), axis=1))
    for t in range(DAYS):
        for copy in days[t]:
            copy.wait()
        for i in range(OWN // 8):
            value = exposed[t, rows(i), :] * jnp.exp(offsets[i] + lat[t, rows(i), :])
            inten[t, rows(i), :] = value
            exc[t, rows(i), :] = value - cnt[t, rows(i), :].astype(jnp.float32)
    last = OWN // 8 - 1
    for t in range(DAYS):
        send(
            t,
            jnp.where(row < 2, up_roll(inten[t, rows(last), :], 2), lat[t, rows(last), :]),
            jnp.where(row >= 6, up_roll(inten[t, rows(0), :], 6), lat[t, rows(0), :]),
        )
    for k in range(DAYS // 2):
        a, b = 2 * k, 2 * k + 1
        send(
            DAYS + k,
            jnp.where(row >= 4, exc[a, rows(last), :], up_roll(exc[b, rows(last), :], 4)),
            jnp.where(row < 4, exc[a, rows(0), :], up_roll(exc[b, rows(0), :], 4)),
        )


def residual_kernel(latent, inten, exc, z_first, z_second, lat, res, inner, y_msg, c_msg, tmp):
    has_above, has_below, has_before, has_after, even = places()
    above, below = edges(z_first, z_second)
    row = row_iota()

    def field(t, i):
        if i in OWN_TILES:
            return latent[t, rows(i - 1), :]
        return (above if i == 0 else below)[rows(t), :]

    same = [(t, t) for t in range(DAYS)]
    apply_k(field, tmp, same, has_above, has_below)
    apply_k(framed(tmp), lat, same, has_above, has_below)
    weight = day_weights(has_before, has_after)

    for i in range(TILES):
        s = [lat[t, rows(i), :] for t in range(DAYS)]
        for t in range(DAYS):
            if i in (0, BOTTOM):
                excess = (above if i == 0 else below)[rows(DAYS + t // 2), :]
                excess = up_roll(excess, 4) if t % 2 else excess
            else:
                excess = exc[t, rows(i - 1), :]
            value = weight[t] * s[t] + excess
            if t > 0:
                value = value - COUPLE * s[t - 1]
            if t < DAYS - 1:
                value = value - COUPLE * s[t + 1]
            res[t, rows(i), :] = -value
    middle = range(DAYS - 2)
    apply_k(framed(res), tmp, [(k + 1, k) for k in middle], has_above, has_below)
    apply_k(framed(tmp), inner, [(k, k) for k in middle], has_above, has_below)

    def send(at, before, after):
        y_msg[rows(at), :] = jnp.where(even, before, after)
        c_msg[rows(at), :] = jnp.where(even, after, before)

    def halo(field, day):
        return jnp.where(row < 4, field[day, rows(BOTTOM), :], field[day, rows(0), :])

    first, last = 0, DAYS - 1
    for i in OWN_TILES:
        send(S_AT + i, lat[first, rows(i), :], lat[last, rows(i), :])
        send(R_AT + i, res[first, rows(i), :], res[last, rows(i), :])
        send(Q_AT + i - 1, -COUPLE * inner[0, rows(i), :], -COUPLE * inner[DAYS - 3, rows(i), :])
        send(I_AT + i - 1, inten[first, rows(i - 1), :], inten[last, rows(i - 1), :])
    send(S_AT, halo(lat, first), halo(lat, last))
    send(R_AT, halo(res, first), halo(res, last))
    outer = (row < 2) | (row >= 6)

    def slim(day, near):
        wanted = jnp.where(row < 4, up_roll(above[rows(day), :], 2), up_roll(below[rows(day), :], 6))
        return jnp.where(outer, -COUPLE * halo(inner, near), wanted)

    send(H_AT, slim(first, 0), slim(last, DAYS - 3))


def image_kernel(
    res, inner, lat, inten, z_first, z_second, y_msg, c_msg, u_out, q_out, z_out, sets, r6, mixed, f6, tmp
):
    has_above, has_below, has_before, has_after, even = places()
    above, below = edges(z_first, z_second)
    weight = day_weights(has_before, has_after)
    last = DAYS + 1

    def got(at):
        y, c = y_msg[rows(at), :], c_msg[rows(at), :]
        return jnp.where(even, y, c), jnp.where(even, c, y)

    for i in range(TILES):
        k = i if i in OWN_TILES else 0
        s_before, s_after = got(S_AT + k)
        r_before, r_after = got(R_AT + k)
        r6[0, rows(i), :] = jnp.where(has_before, r_before + COUPLE * lat[0, rows(i), :], 0.0)
        r6[last, rows(i), :] = jnp.where(has_after, r_after + COUPLE * lat[DAYS - 1, rows(i), :], 0.0)
        r6[1, rows(i), :] = res[0, rows(i), :] + COUPLE * s_before
        r6[DAYS, rows(i), :] = res[DAYS - 1, rows(i), :] + COUPLE * s_after
    outer = [(0, 0), (1, 1), (DAYS, DAYS), (last, last)]
    apply_k(framed(r6), tmp, outer, has_above, has_below)
    apply_k(framed(tmp), f6, outer, has_above, has_below)

    def residual(t, i):
        return r6[t, rows(i), :] if (t, t) in outer else res[t - 1, rows(i), :]

    def intensity(t, i):
        if i in OWN_TILES:
            return inten[t, rows(i - 1), :]
        return up_roll(above[rows(t), :], 6) if i == 0 else up_roll(below[rows(t), :], 2)

    for i in range(TILES):
        f = [
            f6[t, rows(i), :] if (t, t) in outer else inner[t - 2, rows(i), :]
            for t in range(DAYS + 2)
        ]
        r = [residual(t, i) for t in range(DAYS + 2)]
        if i in OWN_TILES:
            q_side, i_side = got(Q_AT + i - 1), got(I_AT + i - 1)
        else:
            q_side = got(H_AT)
            i_side = [up_roll(v, 4) for v in q_side]
        before = INNER * f[0] - COUPLE * f[1] + q_side[0] + i_side[0] * r[0]
        after = INNER * f[last] - COUPLE * f[DAYS] + q_side[1] + i_side[1] * r[last]
        q = [jnp.where(has_before, before, 0.0)]
        for t in range(DAYS):
            q.append(weight[t] * f[t + 1] - COUPLE * (f[t] + f[t + 2]) + intensity(t, i) * r[t + 1])
        q.append(jnp.where(has_after, after, 0.0))
        for t in range(DAYS):
            mixed[t, rows(i), :] = weight[t] * q[t + 1] - COUPLE * (q[t] + q[t + 2])
            if i in OWN_TILES:
                q_out[t, rows(i - 1), :] = q[t + 1]
    days = [(t, t) for t in range(DAYS)]
    apply_k(framed(mixed), tmp, days, has_above, has_below)
    apply_k(framed(tmp), mixed, days, has_above, has_below, OWN_TILES)
    zero = jnp.zeros((8, COLUMNS), jnp.float32)

    uu = uq = zero
    for i in OWN_TILES:
        for t in range(DAYS):
            q, u = q_out[t, rows(i - 1), :], residual(t + 1, i)
            z_out[t, rows(i - 1), :] = mixed[t, rows(i), :] + intensity(t, i) * q
            u_out[t, rows(i - 1), :] = u
            uu = uu + u * u
            uq = uq + u * q

    def total(v):
        return jnp.sum(jnp.sum(v, axis=0, keepdims=True), axis=1, keepdims=True)

    uu, uq = total(uu), total(uq)
    ratio = jnp.where(uu > 0, uq / uu, 0.0)
    uw = ww = uy = wy = zero
    for i in range(OWN // 8):
        for t in range(DAYS):
            u, q, z = u_out[t, rows(i), :], q_out[t, rows(i), :], z_out[t, rows(i), :]
            w = q - ratio * u
            y = z - ratio * q
            uw, ww, uy, wy = uw + u * w, ww + w * w, uy + u * y, wy + w * y
    write_sets(sets, [uu, total(uw), total(ww), total(uy), total(wy), ratio])


def write_sets(sets, values):
    lane = lax.broadcasted_iota(jnp.int32, (1, 128), 1)
    out = jnp.zeros((1, 128), jnp.float32)
    for k, value in enumerate(values):
        out = jnp.where(lane == k, value, out)
    sets[...] = jnp.broadcast_to(out, sets.shape)


def recentred(got):
    by_lane = got[...].T
    uu, uw, ww, uy, wy, ratio = (by_lane[k : k + 1, :] for k in range(6))

    def add(v):
        return jnp.sum(v, axis=1, keepdims=True)

    total = add(uu)
    centre = jnp.where(total > 0, add(uw + ratio * uu) / total, 0.0)
    e = ratio - centre
    uw_new = uw + e * uu
    ww_new = ww + e * (2.0 * uw + e * uu)
    uy_new = uy + e * uw + e * ratio * uu
    wy_new = wy + e * (ww + ratio * uw + uy) + e * e * (uw + ratio * uu)
    return total, add(uw_new), add(ww_new), add(uy_new), add(wy_new), centre


def regroup_kernel(got, sets):
    write_sets(sets, recentred(got))


def update_kernel(got, latent, u_in, q_in, z_in, updated, residual, new, left, sems):
    m0, _, ww, _, wy, centre = recentred(got)
    alpha0 = 1.0 / centre
    norm1 = alpha0 * alpha0 * ww
    beta = norm1 / m0
    curvature1 = alpha0 * alpha0 * wy - beta * beta * (centre * m0)
    alpha1 = norm1 / curvature1
    copies = []
    for t in range(DAYS):
        for i in range(OWN // 8):
            u, q, z = u_in[t, rows(i), :], q_in[t, rows(i), :], z_in[t, rows(i), :]
            residual1 = u - alpha0 * q
            direction1 = residual1 + beta * u
            image1 = (q - alpha0 * z) + beta * q
            new[t, rows(i), :] = latent[t, rows(i), :] + (alpha0 * u + alpha1 * direction1)
            left[t, rows(i), :] = residual1 - alpha1 * image1
        copies += [
            pltpu.make_async_copy(new.at[t], updated.at[t], sems.at[2 * t]),
            pltpu.make_async_copy(left.at[t], residual.at[t], sems.at[2 * t + 1]),
        ]
        copies[-2].start()
        copies[-1].start()
    for copy in copies:
        copy.wait()


def gathered(sets, axis):
    return lax.all_to_all(sets, axis, 0, 0)


def body(latent, counts, exposure, region_ids, coefficients):
    spaces, times = lax.axis_size("space"), lax.axis_size("tm")
    field, four = f32(DAYS, OWN, COLUMNS), f32(DAYS, FRAME, COLUMNS)
    edge, message = f32(EDGE, COLUMNS), f32(8 * MESSAGE_TILES, COLUMNS)

    def vmem(shape, dtype=jnp.float32):
        return pltpu.VMEM(shape, dtype)

    one_hot = region_ids[:, None, None] == jnp.arange(coefficients.shape[0])[None, :, None]
    offset = jnp.where(one_hot, coefficients[None, :, None], 0.0)
    offset = jnp.sum(jnp.broadcast_to(offset, offset.shape[:2] + (128,)), axis=1)

    lat, exc, inten, z_first, z_second = pl.pallas_call(
        intensity_kernel,
        out_shape=(field, field, field, edge, edge),
        in_specs=[VMEM] + [HBM] * 3,
        out_specs=(VMEM,) * 5,
        scratch_shapes=[
            vmem(counts.shape, jnp.int32),
            vmem(exposure.shape),
            pltpu.SemaphoreType.DMA((3 * DAYS,)),
        ],
        compiler_params=FETCHING,
        name="intensity",
    )(offset, latent, counts, exposure)

    def pairs(count, first):
        return [p for i in range(first, count - 1, 2) for p in ((i, i + 1), (i + 1, i))]

    def turns(k):
        return [
            (t * spaces + i, t * spaces + j)
            for t in range(times)
            for i, j in pairs(spaces, (t + k) % 2)
        ]

    z_first = lax.ppermute(z_first, ("tm", "space"), turns(1))
    z_second = lax.ppermute(z_second, ("tm", "space"), turns(0))

    spatial, res, inner, y_msg, c_msg = pl.pallas_call(
        residual_kernel,
        out_shape=(four, four, f32(DAYS - 2, FRAME, COLUMNS), message, message),
        in_specs=[VMEM] * 5,
        out_specs=(VMEM,) * 5,
        scratch_shapes=[vmem(four.shape)],
        compiler_params=PARAMS,
        name="residual",
    )(lat, inten, exc, z_first, z_second)

    y_got = lax.ppermute(y_msg, "tm", pairs(times, 1))
    c_got = lax.ppermute(c_msg, "tm", pairs(times, 0))

    six = vmem((DAYS + 2, FRAME, COLUMNS))
    u, q, z, sets = pl.pallas_call(
        image_kernel,
        out_shape=(field, field, field, f32(times, 128)),
        in_specs=[VMEM] * 8,
        out_specs=(VMEM,) * 4,
        scratch_shapes=[six] * 4,
        compiler_params=PARAMS,
        name="image",
    )(res, inner, spatial, inten, z_first, z_second, y_got, c_got)

    sets = pl.pallas_call(
        regroup_kernel,
        out_shape=f32(spaces, 128),
        in_specs=[VMEM],
        out_specs=VMEM,
        compiler_params=PARAMS,
        name="regroup",
    )(gathered(sets, "tm"))

    return pl.pallas_call(
        update_kernel,
        out_shape=(field, field),
        in_specs=[VMEM] * 5,
        out_specs=(HBM, HBM),
        scratch_shapes=[
            vmem(latent.shape),
            vmem(latent.shape),
            pltpu.SemaphoreType.DMA((2 * DAYS,)),
        ],
        compiler_params=PARAMS,
        name="update",
    )(gathered(sets, "space"), latent, u, q, z)


def solution(mesh):
    return jax.shard_map(
        body,
        mesh=mesh,
        in_specs=(
            P("tm", "space", None),
            P("tm", "space", None),
            P("tm", "space", None),
            P("space"),
            P(),
        ),
        out_specs=(P("tm", "space", None), P("tm", "space", None)),
        check_vma=False,
    )
```
